128 devices in a mesh: row: 16 (over z_lo, x, core), col: 8 (over y, z_hi).
Axes of the slice: x: 4, y: 4, z: 4 (z_hi: 2, z_lo: 2; z = z_hi * 2 + z_lo), core: 2. Of those that a mesh axis runs over, the one named last changes fastest.
Arguments:
- crossings: bfloat16 [6144, 2, 128, 128], P(('row', 'col')), may hold values from -50 to 50
- counts: int32 [8, 16], P('col', 'row'), may hold values from 1 to 48, 192 in all within a row
- dest: int32 [128, 48], P(('row', 'col')), may hold values from 0 to 47, each once within a row
Outputs:
- scores: float32 [1536, 1536], P('row', 'col')
The draws below stay inside these ranges and needn't reach their ends.
Inputs may be any that keep to these rules, and one draw needn't show every extreme that they name: In every column c the counts add up to 192, and one shard of every column holds exactly 48. `dest`: each shard's row is a permutation.
All inputs are finite; a program needn't handle non-finite values.
Results may differ from the reference program's by a relative error of at most 0.00075.
Values may be sent and summed in bfloat16 or wider, within the bound.
A program may use at most 192 MiB of HBM per device.

```python
import math
import jax
import jax.numpy as jnp
import numpy as np
from jax import lax

NX = 128
NZ = 128
M = 12
SLOTS = 48
SHARD_ROWS = 16
SHARD_COLS = 8
ALL_SLOTS = 6144
CROSSINGS = 1536


def draw_crossings(key, part):
    noise_key, scale_key = jax.random.split(key, 2)
    full_shape = (ALL_SLOTS, 2, NZ, NX)
    jitter = jnp.clip(jax.random.normal(noise_key, full_shape, jnp.float32), -5.0, 5.0)
    scales = jnp.exp(jax.random.uniform(scale_key, (ALL_SLOTS, 2, NZ, 1), jnp.float32, 0.0, math.log(10.0)))
    values = scales * jitter
    return values.astype(jnp.bfloat16)


def split_up(count, total, most, skew):
    loads = [(1 << 20) // math.isqrt(grade ** skew) + 1 for grade in range(2, count + 1)]
    spare, given = total - most - (count - 1), [1] * (count - 1)
    while spare > 0:
        candidates = [i for i in range(count - 1) if given[i] < most]
        pool, remaining = sum([loads[i] for i in candidates]), spare
        for i in candidates:
            more = min(most - given[i], max(1, remaining * loads[i] // pool), spare)
            given[i] = given[i] + more
            spare = spare - more
    return np.array([most] + given)


def ragged(stream_key, number_of, total, limit, slope):
    if number_of == 2:
        one = jax.random.randint(stream_key, (), max(1, total - limit), min(limit, total - 1) + 1)
        return jnp.stack([one, total - one])
    tallies = jnp.asarray(split_up(number_of, total, limit, slope), jnp.int32)
    couples = (number_of - 1) // 2
    donor, sink = tallies[1:1 + 2 * couples:2], tallies[2:2 + 2 * couples:2]
    slack = jnp.minimum(donor - 1, limit - sink)
    moved = jax.random.randint(jax.random.fold_in(stream_key, 1), (couples,), 0, 1 << 20) % (slack + 1)
    tallies = tallies.at[1:1 + 2 * couples:2].set(donor - moved).at[2:2 + 2 * couples:2].set(sink + moved)
    return tallies[jax.random.permutation(jax.random.fold_in(stream_key, 2), number_of)]


def setup_inputs(seed: int = 0) -> dict:
    streams_of = jax.random.split(jax.random.key(seed), 4)
    return {
        "crossings": draw_crossings(jax.random.fold_in(streams_of[3], 71), 0),
        "counts": jax.vmap(lambda own: ragged(own, SHARD_ROWS, SHARD_ROWS * M, SLOTS, 2))(jax.random.split(streams_of[1], SHARD_COLS)).reshape((SHARD_COLS, SHARD_ROWS)).astype(jnp.int32),
        "dest": jax.vmap(lambda own: jax.random.permutation(own, SLOTS))(jax.random.split(streams_of[2], (SHARD_ROWS * SHARD_COLS))).reshape((SHARD_ROWS * SHARD_COLS, SLOTS)).astype(jnp.int32),
    }


epsilon = 1e-06

def inverse_table(points):
    row_ids = jnp.arange(points, dtype=jnp.int32)[:, None]
    col_ids = jnp.arange(points, dtype=jnp.int32)[None, :]
    halfway = points // 2
    wavenumber = jnp.where(row_ids <= halfway, row_ids, row_ids - halfway)
    phases = wavenumber * col_ids % points
    angles = phases.astype(jnp.float32) * (2.0 * math.pi / points)
    weight = jnp.where((row_ids == 0) | (row_ids == halfway), 1.0, 2.0)
    values = jnp.where(row_ids <= halfway, weight * jnp.cos(angles), -2.0 * jnp.sin(angles)) / points
    return values.astype(jnp.float32)

def reflect(coeffs):
    count_rows, points, feature_width = coeffs.shape
    split_view = coeffs.reshape(count_rows, points, 2, feature_width // 2)
    mirrored = jnp.roll(jnp.flip(split_view, -1), 1, -1)
    mirrored = jnp.concatenate([mirrored[:, :, :1], -mirrored[:, :, 1:]], 2)
    return mirrored.reshape(count_rows, points, feature_width)

def energy(coeffs):
    points = coeffs.shape[1]
    halfway = points // 2
    index_ids = jnp.arange(points, dtype=jnp.int32)
    weights = jnp.where((index_ids == 0) | (index_ids == halfway), 1.0, 2.0).astype(jnp.float32)
    squares = lax.optimization_barrier(jnp.sum(jnp.square(coeffs.astype(jnp.float32)), -1))
    return jnp.dot(squares, weights, precision=lax.Precision.HIGHEST) / (points * points * coeffs.shape[2])

def pair_scores(leading, lead_energy, trailing, trail_energy, shift_table):
    halfway = leading.shape[1] // 2
    lead_rows = leading.shape[0]
    entries = leading.shape[1] * leading.shape[2]
    doubled = jnp.concatenate([leading, reflect(leading)], 0).astype(jnp.float32)
    highest_prec = lax.Precision.HIGHEST
    real_lead = doubled[:, :halfway + 1]
    imag_lead = doubled[:, halfway + 1:]
    real_trail = trailing[:, :halfway + 1]
    imag_trail = trailing[:, halfway + 1:]
    real_real = jnp.einsum('akq,bkq->kab', real_lead, real_trail, precision=highest_prec)
    imag_imag = jnp.einsum('akq,bkq->kab', imag_lead, imag_trail, precision=highest_prec)
    real_imag = jnp.einsum('akq,bkq->kab', real_lead[:, 1:halfway], imag_trail, precision=highest_prec)
    imag_real = jnp.einsum('akq,bkq->kab', imag_lead, real_trail[:, 1:halfway], precision=highest_prec)
    gram_terms = jnp.concatenate([real_real[:1], real_real[1:halfway] + imag_imag, real_real[halfway:], real_imag - imag_real], 0)
    shifted = jnp.einsum('jab,js->abs', gram_terms, shift_table, precision=highest_prec)
    excess = lax.optimization_barrier(jnp.max(shifted - lax.optimization_barrier(jnp.mean(shifted, -1, keepdims=True)), -1))
    highest = jnp.maximum(excess[:lead_rows], excess[lead_rows:])
    return highest / (math.sqrt(entries) * jnp.sqrt(lead_energy + epsilon)[:, None] * jnp.sqrt(trail_energy + epsilon)[None, :])

def reference(crossings, counts, dest):
    shard_total = SHARD_ROWS * SHARD_COLS
    shard_counts = jnp.transpose(counts).reshape(shard_total).astype(jnp.int32)
    offsets = (jnp.cumsum(counts, axis=1) - counts).astype(jnp.int32)
    shard_offsets = jnp.transpose(offsets).reshape(shard_total)
    is_live = dest < shard_counts[:, None]
    ordinal = (shard_offsets[:, None] + dest).astype(jnp.int32)
    owner_row = ordinal % SHARD_ROWS
    placed = ordinal // SHARD_ROWS
    column = (jnp.arange(shard_total, dtype=jnp.int32) % SHARD_COLS)[:, None]
    target = (owner_row * SHARD_COLS + column) * M + placed
    target = jnp.where(is_live, target, CROSSINGS).reshape(-1).astype(jnp.int32)
    ordered = jnp.zeros((CROSSINGS, 2, NZ, NX), jnp.bfloat16).at[target].set(crossings, mode='drop')
    spectrum = jnp.fft.rfft(ordered.astype(jnp.float32), axis=-1)
    halfway = NX // 2
    stacked = jnp.concatenate([jnp.real(spectrum), jnp.imag(spectrum)[..., 1:halfway]], -1)
    coeffs = jnp.transpose(stacked, (0, 3, 1, 2)).reshape(CROSSINGS, NX, 2 * NZ).astype(jnp.bfloat16)
    energies = energy(coeffs)
    col_coeffs = jnp.transpose(coeffs.reshape(SHARD_ROWS, SHARD_COLS, M, NX, 2 * NZ), (1, 0, 2, 3, 4)).reshape(CROSSINGS, NX, 2 * NZ)
    col_energy = jnp.transpose(energies.reshape(SHARD_ROWS, SHARD_COLS, M), (1, 0, 2)).reshape(CROSSINGS)
    col_wide = col_coeffs.astype(jnp.float32)
    shift_table = inverse_table(NX)
    row_blocks = coeffs.reshape(SHARD_ROWS, SHARD_COLS * M, NX, 2 * NZ)
    row_energies = energies.reshape(SHARD_ROWS, SHARD_COLS * M)

    def score_block(block_pair):
        return pair_scores(block_pair[0], block_pair[1], col_wide, col_energy, shift_table)
    blocks = lax.map(score_block, (row_blocks, row_energies))
    return blocks.reshape(CROSSINGS, CROSSINGS)
```

```python
import math

import jax
import jax.numpy as jnp
import ml_dtypes
import numpy as np
from jax import lax
from jax.experimental import pallas as pl
from jax.experimental.pallas import tpu as pltpu
from jax.sharding import PartitionSpec as P

M = 12
NX = 128
ENTRIES = 256
ROWS = 16
COLS = 8
BUCKETS = 3
PARTS = 8
PITCH = 200

epsilon = 1e-06

MESH = pl.DeviceIdType.MESH
NT = (((1,), (1,)), ((), ()))
f32 = jnp.float32
bf16 = jnp.bfloat16


def split3(table):
    high = table.astype(ml_dtypes.bfloat16)
    rest = table - high.astype(np.float64)
    mid = rest.astype(ml_dtypes.bfloat16)
    low = (rest - mid.astype(np.float64)).astype(ml_dtypes.bfloat16)
    return high, mid, low


def tables():
    rows = np.arange(NX)
    part, inner = rows // 16, rows % 16
    wave = part * 8 + inner % 8
    imaginary = (inner >= 8) & (wave > 0)
    wave = np.where((inner >= 8) & (wave == 0), NX // 2, wave)
    points = np.arange(NX)
    angles = 2.0 * math.pi * ((wave[:, None] * points[None, :]) % NX) / NX
    forward = np.where(imaginary[:, None], -np.sin(angles), np.cos(angles))
    weight = np.where((wave == 0) | (wave == NX // 2), 1.0, 2.0)[:, None]
    inverse = weight * np.where(imaginary[:, None], -np.sin(angles), np.cos(angles)) / NX
    inverse = inverse - inverse.mean(1, keepdims=True)
    f_high, f_mid, f_low = split3(forward)
    forward_stack = np.concatenate([f_high, f_mid, f_low], 0)
    i_high, i_mid, _ = split3(inverse.T)
    shift = np.block([[i_high, i_high], [i_mid, np.zeros_like(i_mid)]])
    swap = np.zeros((256, 256))
    for first in range(16):
        for second in range(16):
            swap[first * 16 + second, second * 16 + first] = 1.0
    mirror = np.zeros((ENTRIES, ENTRIES))
    for point in range(128):
        mirror[(-point) % 128, point] = 1.0
        mirror[128 + (-point) % 128, 128 + point] = -1.0
    return (
        forward_stack.astype(ml_dtypes.bfloat16),
        swap.astype(ml_dtypes.bfloat16),
        mirror.astype(ml_dtypes.bfloat16),
        shift.astype(ml_dtypes.bfloat16),
    )


def dot_nt(a, b):
    return lax.dot_general(a, b, NT, preferred_element_type=f32)


def place():
    r = lax.axis_index("row")
    c = lax.axis_index("col")
    return r // 8, (r // 2) % 4, r % 2, c // 2, c % 2


def score_kernel(
    picks, planes, forward, swap, mirror, shift, out,
    cols, leads, y_lead, y_col, gram_a, gram_b, e_lead, e_col, send, recv,
):
    z, x, k, y, h = place()
    my_row = z * 8 + x * 2 + k
    my_col = y * 2 + h

    def row_at(dz, dx, dk=0):
        return ((z + dz) % 2) * 8 + ((x + dx) % 4) * 2 + (k + dk) % 2

    def col_at(dh, dy):
        return ((y + dy) % 4) * 2 + (h + dh) % 2

    sib, zl = (row_at(0, 0, 1), my_col), (row_at(1, 0), my_col)
    xp, xm = (row_at(0, 1), my_col), (row_at(0, 3), my_col)
    zh, yp, ym = (my_row, col_at(1, 0)), (my_row, col_at(0, 1)), (my_row, col_at(0, 3))

    barrier = pltpu.get_barrier_semaphore()
    for device in (sib, zl, xp, xm, zh, yp, ym):
        pl.semaphore_signal(barrier, inc=1, device_id=device, device_id_type=MESH)
    pl.semaphore_wait(barrier, 7)

    def transform(p, _):
        parts = dot_nt(forward[...], planes[picks[p]])
        value = (parts[:NX] + (parts[NX : 2 * NX] + parts[2 * NX :])).astype(bf16)
        cols[my_row, p] = value
        leads[my_col, p] = value
        return 0

    lax.fori_loop(0, M, transform, 0)

    def piece(ref, slot, t):
        return ref.at[slot, :, pl.ds(pl.multiple_of(t * 16, 16), 16), :]

    def copy(flow, ref, slot, t, device):
        block = piece(ref, slot, t)
        return pltpu.make_async_remote_copy(
            src_ref=block,
            dst_ref=block,
            send_sem=send.at[flow, t],
            recv_sem=recv.at[flow, t],
            device_id=device,
            device_id_type=MESH,
        )

    own_c, own_l = row_at(0, 0), col_at(0, 0)
    sends = {
        0: (cols, own_c, zl), 1: (cols, own_c, xp), 3: (cols, own_c, xm), 7: (cols, own_c, sib),
        2: (cols, row_at(1, 0), xp), 4: (cols, row_at(1, 0), xm), 8: (cols, row_at(1, 0), sib),
        5: (cols, row_at(0, 3), xp), 9: (cols, row_at(0, 3), sib), 10: (cols, row_at(1, 3), sib),
        11: (cols, row_at(0, 1), sib), 6: (cols, row_at(1, 1), xm), 12: (cols, row_at(1, 1), sib),
        13: (cols, row_at(0, 2), sib), 14: (cols, row_at(1, 2), sib),
        15: (leads, own_l, zh), 16: (leads, own_l, yp), 18: (leads, own_l, ym),
        17: (leads, col_at(1, 0), yp), 19: (leads, col_at(1, 0), ym),
        20: (leads, col_at(0, 3), yp), 21: (leads, col_at(1, 1), ym),
    }
    arrives = {
        0: row_at(1, 0), 1: row_at(0, 3), 2: row_at(1, 3), 3: row_at(0, 1), 4: row_at(1, 1),
        5: row_at(0, 2), 6: row_at(1, 2),
        7: row_at(0, 0, 1), 8: row_at(1, 0, 1), 9: row_at(0, 3, 1), 10: row_at(1, 3, 1),
        11: row_at(0, 1, 1), 12: row_at(1, 1, 1), 13: row_at(0, 2, 1), 14: row_at(1, 2, 1),
        15: col_at(1, 0), 16: col_at(0, 3), 17: col_at(1, 3), 18: col_at(0, 1), 19: col_at(1, 1),
        20: col_at(0, 2), 21: col_at(1, 2),
    }

    def start(flows, t):
        for flow in flows:
            ref, slot, device = sends[flow]
            copy(flow, ref, slot, t, device).start()

    def wait_in(flows, t):
        for flow in flows:
            ref, _, device = sends[flow]
            copy(flow, ref, arrives[flow], t, device).wait_recv()

    e_lead[...] = jnp.zeros_like(e_lead)
    e_col[...] = jnp.zeros_like(e_col)

    def score_part(t):
        r0 = pl.ds(pl.multiple_of(t * 16, 16), 16)
        order = swap[...]

        def relay(ref, groups, dst):
            flat = ref.reshape(groups * 16, NX, ENTRIES)
            for g in range(groups):
                block = flat[g * 16 : (g + 1) * 16, r0, :].reshape(256, ENTRIES)
                turned = jnp.dot(order, block, preferred_element_type=f32).astype(bf16)
                dst[:, g * 16 : (g + 1) * 16, :] = turned.reshape(16, 16, ENTRIES)

        relay(leads, 6, y_lead)
        relay(cols, 12, y_col)
        first = jnp.where(t == 0, 1.0, 0.0).astype(f32)
        for dst, source, count in ((e_lead, y_lead, 96), (e_col, y_col, 192)):
            total = dst[...]
            for j in range(16):
                value = source[j, :count, :].astype(f32)
                square = value * value
                square = square[:, :128] + square[:, 128:]
                weight = (2.0 - first) if j % 8 == 0 else 2.0
                total = total + weight * square
            dst[...] = total
        turn = mirror[...]
        for j in range(16):
            y_lead[j, 96:, :] = jnp.dot(y_lead[j, :96, :], turn, preferred_element_type=f32).astype(bf16)
        for i in range(8):
            lr, li, tr, ti = y_lead[i], y_lead[8 + i], y_col[i], y_col[8 + i]
            rr, ii, ri, ir = dot_nt(lr, tr), dot_nt(li, ti), dot_nt(lr, ti), dot_nt(li, tr)
            if i == 0:
                real = rr + (1.0 - first) * ii
                imag = first * ii + (1.0 - first) * (ri - ir)
            else:
                real, imag = rr + ii, ri - ir
            for value, j in ((real, i), (imag, 8 + i)):
                base = pl.ds(pl.multiple_of((t * 16 + j) * PITCH, 8), 192)
                gram_a[base, :] = value[:, :128]
                gram_b[base, :64] = value[:, 128:]

    def step(s, _):
        @pl.when(s < PARTS)
        def _():
            start((0, 1, 3, 15, 16, 18, 7), s)

        @pl.when((s >= 1) & (s < PARTS + 1))
        def _():
            wait_in((0, 15), s - 1)
            start((2, 4, 17, 19, 8), s - 1)

        @pl.when((s >= 2) & (s < PARTS + 2))
        def _():
            wait_in((1, 4, 16, 19), s - 2)
            start((5, 6, 20, 21, 9, 12), s - 2)
            wait_in((2, 3), s - 2)
            start((10, 11), s - 2)

        @pl.when((s >= 3) & (s < PARTS + 3))
        def _():
            wait_in((5, 6), s - 3)
            start((13, 14), s - 3)

        @pl.when(s >= 4)
        def _():
            wait_in((17, 18, 20, 21, 7, 8, 9, 10, 11, 12, 13, 14), s - 4)
            score_part(s - 4)

        return 0

    lax.fori_loop(0, PARTS + 4, step, 0)

    scale_lead = jnp.sqrt(jnp.sum(e_lead[...], -1, keepdims=True) / (NX * NX * ENTRIES) + epsilon)
    ones = jnp.ones((8, 128), f32)
    across = lax.dot_general(ones, e_col[...], NT, precision=lax.Precision.HIGHEST, preferred_element_type=f32)
    scale_col = jnp.sqrt(across[:1] / (NX * NX * ENTRIES) + epsilon)
    e_lead[...] = jnp.broadcast_to(scale_lead, (96, 128))
    to_shift = shift[...]

    def best(b, _):
        found = []
        for u in range(8):
            a = b * 8 + u
            values = []
            for start_row in (a, a + 96):
                values.append(gram_a[pl.ds(start_row, NX, stride=PITCH), :])
                values.append(gram_b[pl.ds(start_row, NX, stride=PITCH), :][:, :64])
            value = jnp.concatenate(values, 1)
            high = value.astype(bf16)
            low = (value - high.astype(f32)).astype(bf16)
            moved = jnp.dot(to_shift, jnp.concatenate([high, low], 0), preferred_element_type=f32)
            top = jnp.max(moved[:NX] + moved[NX:], axis=0, keepdims=True)
            found.append(jnp.maximum(top[:, :192], top[:, 192:]))
        rows = pl.ds(pl.multiple_of(b * 8, 8), 8)
        scale = e_lead[rows, :]
        scale = jnp.concatenate([scale, scale[:, :64]], 1)
        out[rows, :] = jnp.concatenate(found, 0) / (math.sqrt(NX * ENTRIES) * scale * scale_col)
        return 0

    lax.fori_loop(0, 96 // 8, best, 0)

    def finish(t, _):
        for flow, (ref, slot, device) in sends.items():
            copy(flow, ref, slot, t, device).wait_send()
        return 0

    lax.fori_loop(0, PARTS, finish, 0)


def scores_of(picks, planes):
    vmem = pl.BlockSpec(memory_space=pltpu.VMEM)
    return pl.pallas_call(
        score_kernel,
        out_shape=jax.ShapeDtypeStruct((COLS * M, ROWS * M), f32),
        in_specs=[pl.BlockSpec(memory_space=pltpu.SMEM)] + [vmem] * 5,
        out_specs=vmem,
        scratch_shapes=[
            pltpu.VMEM((ROWS, M, NX, ENTRIES), bf16),
            pltpu.VMEM((COLS, M, NX, ENTRIES), bf16),
            pltpu.VMEM((16, 192, ENTRIES), bf16),
            pltpu.VMEM((16, 192, ENTRIES), bf16),
            pltpu.VMEM((NX * PITCH, 128), f32),
            pltpu.VMEM((NX * PITCH, 128), f32),
            pltpu.VMEM((96, 128), f32),
            pltpu.VMEM((192, 128), f32),
            pltpu.SemaphoreType.DMA((22, PARTS)),
            pltpu.SemaphoreType.DMA((22, PARTS)),
        ],
        compiler_params=pltpu.CompilerParams(
            collective_id=1, has_side_effects=True, vmem_limit_bytes=60 * 2**20
        ),
        name="scores",
    )(picks, planes, *[jnp.asarray(table) for table in tables()])


def body(crossings, counts, dest):
    my_row = lax.axis_index("row")
    slot_total = crossings.shape[0]
    shard_counts = lax.all_gather(counts, "row", axis=1, tiled=True).reshape(ROWS)
    source_ids = jnp.arange(ROWS, dtype=jnp.int32)
    offsets = jnp.sum(jnp.where(source_ids[None, :] < source_ids[:, None], shard_counts[None, :], 0), 1)
    my_offset = jnp.sum(jnp.where(source_ids < my_row, shard_counts, 0))
    slot_ids = jnp.arange(slot_total, dtype=jnp.int32)
    buckets = jnp.arange(BUCKETS, dtype=jnp.int32)[None, :]
    outgoing = (buckets * ROWS + (source_ids[:, None] - my_offset) % ROWS).reshape(-1)
    chosen = jnp.sum(jnp.where(dest.reshape(1, -1) == outgoing[:, None], slot_ids[None, :], 0), 1)
    payload = crossings.reshape(slot_total, -1)[chosen].reshape(ROWS, BUCKETS, ENTRIES, NX)
    received = lax.all_to_all(payload, "row", split_axis=0, concat_axis=0, tiled=True)
    wanted = jnp.arange(M, dtype=jnp.int32)[:, None] * ROWS + my_row
    within = wanted - offsets[None, :]
    hit = (within >= 0) & (within < shard_counts[None, :])
    picks = jnp.sum(jnp.where(hit, source_ids[None, :] * BUCKETS + within // ROWS, 0), 1)
    return scores_of(picks, received.reshape(slot_total, ENTRIES, NX))


def solution(mesh):
    return jax.shard_map(
        body,
        mesh=mesh,
        in_specs=(P(("row", "col"), None, None, None), P("col", "row"), P(("row", "col"), None)),
        out_specs=P("row", "col"),
        check_vma=False,
    )
```

```python
import math

import jax
import jax.numpy as jnp
import ml_dtypes
import numpy as np
from jax import lax
from jax.experimental import pallas as pl
from jax.experimental.pallas import tpu as pltpu
from jax.sharding import PartitionSpec as P

M = 12
NX = 128
ENTRIES = 256
ROWS = 16
COLS = 8
BUCKETS = 3
PARTS = 8
PITCH = 200

epsilon = 1e-06

MESH = pl.DeviceIdType.MESH
NT = (((1,), (1,)), ((), ()))
f32 = jnp.float32
bf16 = jnp.bfloat16


def split3(table):
    high = table.astype(ml_dtypes.bfloat16)
    rest = table - high.astype(np.float64)
    mid = rest.astype(ml_dtypes.bfloat16)
    low = (rest - mid.astype(np.float64)).astype(ml_dtypes.bfloat16)
    return high, mid, low


def tables():
    rows = np.arange(NX)
    part, inner = rows // 16, rows % 16
    wave = part * 8 + inner % 8
    imaginary = (inner >= 8) & (wave > 0)
    wave = np.where((inner >= 8) & (wave == 0), NX // 2, wave)
    points = np.arange(NX)
    angles = 2.0 * math.pi * ((wave[:, None] * points[None, :]) % NX) / NX
    forward = np.where(imaginary[:, None], -np.sin(angles), np.cos(angles))
    weight = np.where((wave == 0) | (wave == NX // 2), 1.0, 2.0)[:, None]
    inverse = weight * np.where(imaginary[:, None], -np.sin(angles), np.cos(angles)) / NX
    inverse = inverse - inverse.mean(1, keepdims=True)
    f_high, f_mid, f_low = split3(forward)
    forward_stack = np.concatenate([f_high, f_mid, f_low], 0)
    i_high, i_mid, _ = split3(inverse.T)
    shift = np.block([[i_high, i_high], [i_mid, np.zeros_like(i_mid)]])
    swap = np.zeros((256, 256))
    for first in range(16):
        for second in range(16):
            swap[first * 16 + second, second * 16 + first] = 1.0
    mirror = np.zeros((ENTRIES, ENTRIES))
    for point in range(128):
        mirror[(-point) % 128, point] = 1.0
        mirror[128 + (-point) % 128, 128 + point] = -1.0
    return (
        forward_stack.astype(ml_dtypes.bfloat16),
        swap.astype(ml_dtypes.bfloat16),
        mirror.astype(ml_dtypes.bfloat16),
        shift.astype(ml_dtypes.bfloat16),
    )


def dot_nt(a, b):
    return lax.dot_general(a, b, NT, preferred_element_type=f32)


def place():
    r = lax.axis_index("row")
    c = lax.axis_index("col")
    return r // 8, (r // 2) % 4, r % 2, c // 2, c % 2


OTHERS = [
    (1, 2, 0), (1, 2, 1), (0, 2, 0), (0, 2, 1), (1, 1, 0), (1, 3, 0), (1, 1, 1), (1, 3, 1),
    (0, 1, 0), (0, 3, 0), (0, 1, 1), (0, 3, 1), (1, 0, 0), (1, 0, 1), (0, 0, 1),
]


def score_kernel(
    count, slots, crossings, forward, swap, mirror, shift, out,
    held, staged, planes, tallies, tally, picks, cols, leads, y_lead, y_col, gram_a, gram_b, e_lead, e_col,
    load, tally_sem, send, recv, hand_out, hand_in, count_out, count_in,
):
    fetch = pltpu.make_async_copy(crossings, held, load)
    fetch.start()
    z, x, k, y, h = place()
    my_row = z * 8 + x * 2 + k
    my_col = y * 2 + h

    def row_at(dz, dx, dk=0):
        return ((z + dz) % 2) * 8 + ((x + dx) % 4) * 2 + (k + dk) % 2

    def col_at(dh, dy):
        return ((y + dy) % 4) * 2 + (h + dh) % 2

    sib, zl = (row_at(0, 0, 1), my_col), (row_at(1, 0), my_col)
    xp, xm = (row_at(0, 1), my_col), (row_at(0, 3), my_col)
    zh, yp, ym = (my_row, col_at(1, 0)), (my_row, col_at(0, 1)), (my_row, col_at(0, 3))

    barrier = pltpu.get_barrier_semaphore()
    others = [(row_at(*step), my_col) for step in OTHERS]
    for device in others + [zh, yp, ym]:
        pl.semaphore_signal(barrier, inc=1, device_id=device, device_id_type=MESH)
    tallies[my_row] = jnp.full((8, 128), count[0, 0], jnp.int32)
    pl.semaphore_wait(barrier, len(OTHERS) + 3)

    def tell(e, row, device):
        return pltpu.make_async_remote_copy(
            src_ref=tallies.at[row],
            dst_ref=tallies.at[row],
            send_sem=count_out.at[e],
            recv_sem=count_in.at[e],
            device_id=device,
            device_id_type=MESH,
        )

    def hand(e, row, source, device):
        return pltpu.make_async_remote_copy(
            src_ref=staged.at[row],
            dst_ref=planes.at[source],
            send_sem=hand_out.at[e],
            recv_sem=hand_in.at[e],
            device_id=device,
            device_id_type=MESH,
        )

    senders = [row_at(dz, -dx, dk) for dz, dx, dk in OTHERS]
    for e, device in enumerate(others):
        tell(e, my_row, device).start()
    for e, device in enumerate(others):
        tell(e, senders[e], device).wait_recv()
    to_scalar = pltpu.make_async_copy(tallies, tally, tally_sem)
    to_scalar.start()
    fetch.wait()
    to_scalar.wait()
    my_offset = jnp.int32(0)
    for r in range(ROWS):
        my_offset = my_offset + jnp.where(r < my_row, tally[r, 0, 0], 0)

    for e, device in enumerate(others):
        target = device[0]
        for t in range(BUCKETS):
            staged[target, t] = held[slots[t * ROWS + (target + 256 * ROWS - my_offset) % ROWS]]
        hand(e, target, my_row, device).start()
    for t in range(BUCKETS):
        planes[my_row, t] = held[slots[t * ROWS + (my_row + 256 * ROWS - my_offset) % ROWS]]

    def pick(p, _):
        wanted = p * ROWS + my_row
        offset, found = jnp.int32(0), jnp.int32(0)
        for r in range(ROWS):
            within = wanted - offset
            hit = (within >= 0) & (within < tally[r, 0, 0])
            found = jnp.where(hit, r * BUCKETS + within // ROWS, found)
            offset = offset + tally[r, 0, 0]
        picks[p] = found
        return 0

    lax.fori_loop(0, M, pick, 0)
    for e, device in enumerate(others):
        hand(e, others[e][0], senders[e], device).wait_recv()

    def transform(b, _):
        for u in range(3):
            p = b * 3 + u
            source = picks[p]
            parts = dot_nt(forward[...], planes[source // BUCKETS, source % BUCKETS])
            value = (parts[:NX] + (parts[NX : 2 * NX] + parts[2 * NX :])).astype(bf16)
            cols[my_row, p] = value
            leads[my_col, p] = value
        return 0

    lax.fori_loop(0, M // 3, transform, 0)

    def piece(ref, slot, t):
        return ref.at[slot, :, pl.ds(pl.multiple_of(t * 16, 16), 16), :]

    def copy(flow, ref, slot, t, device):
        block = piece(ref, slot, t)
        return pltpu.make_async_remote_copy(
            src_ref=block,
            dst_ref=block,
            send_sem=send.at[flow, t],
            recv_sem=recv.at[flow, t],
            device_id=device,
            device_id_type=MESH,
        )

    own_c, own_l = row_at(0, 0), col_at(0, 0)
    sends = {
        0: (cols, own_c, zl), 1: (cols, own_c, xp), 3: (cols, own_c, xm), 7: (cols, own_c, sib),
        2: (cols, row_at(1, 0), xp), 4: (cols, row_at(1, 0), xm), 8: (cols, row_at(1, 0), sib),
        5: (cols, row_at(0, 3), xp), 9: (cols, row_at(0, 3), sib), 10: (cols, row_at(1, 3), sib),
        11: (cols, row_at(0, 1), sib), 6: (cols, row_at(1, 1), xm), 12: (cols, row_at(1, 1), sib),
        13: (cols, row_at(0, 2), sib), 14: (cols, row_at(1, 2), sib),
        15: (leads, own_l, zh), 16: (leads, own_l, yp), 18: (leads, own_l, ym),
        17: (leads, col_at(1, 0), yp), 19: (leads, col_at(1, 0), ym),
        20: (leads, col_at(0, 3), yp), 21: (leads, col_at(1, 1), ym),
    }
    arrives = {
        0: row_at(1, 0), 1: row_at(0, 3), 2: row_at(1, 3), 3: row_at(0, 1), 4: row_at(1, 1),
        5: row_at(0, 2), 6: row_at(1, 2),
        7: row_at(0, 0, 1), 8: row_at(1, 0, 1), 9: row_at(0, 3, 1), 10: row_at(1, 3, 1),
        11: row_at(0, 1, 1), 12: row_at(1, 1, 1), 13: row_at(0, 2, 1), 14: row_at(1, 2, 1),
        15: col_at(1, 0), 16: col_at(0, 3), 17: col_at(1, 3), 18: col_at(0, 1), 19: col_at(1, 1),
        20: col_at(0, 2), 21: col_at(1, 2),
    }

    def start(flows, t):
        for flow in flows:
            ref, slot, device = sends[flow]
            copy(flow, ref, slot, t, device).start()

    def wait_in(flows, t):
        for flow in flows:
            ref, _, device = sends[flow]
            copy(flow, ref, arrives[flow], t, device).wait_recv()

    e_lead[...] = jnp.zeros_like(e_lead)
    e_col[...] = jnp.zeros_like(e_col)

    def score_part(t):
        r0 = pl.ds(pl.multiple_of(t * 16, 16), 16)
        order = swap[...]

        def relay(ref, groups, dst):
            flat = ref.reshape(groups * 16, NX, ENTRIES)
            for g in range(groups):
                block = flat[g * 16 : (g + 1) * 16, r0, :].reshape(256, ENTRIES)
                turned = jnp.dot(order, block, preferred_element_type=f32).astype(bf16)
                dst[:, g * 16 : (g + 1) * 16, :] = turned.reshape(16, 16, ENTRIES)

        relay(leads, 6, y_lead)
        relay(cols, 12, y_col)
        first = jnp.where(t == 0, 1.0, 0.0).astype(f32)
        for dst, source, count in ((e_lead, y_lead, 96), (e_col, y_col, 192)):
            total = dst[...]
            for j in range(16):
                value = source[j, :count, :].astype(f32)
                square = value * value
                square = square[:, :128] + square[:, 128:]
                weight = (2.0 - first) if j % 8 == 0 else 2.0
                total = total + weight * square
            dst[...] = total
        turn = mirror[...]
        for j in range(16):
            y_lead[j, 96:, :] = jnp.dot(y_lead[j, :96, :], turn, preferred_element_type=f32).astype(bf16)
        for i in range(8):
            lr, li, tr, ti = y_lead[i], y_lead[8 + i], y_col[i], y_col[8 + i]
            rr, ii, ri, ir = dot_nt(lr, tr), dot_nt(li, ti), dot_nt(lr, ti), dot_nt(li, tr)
            if i == 0:
                real = rr + (1.0 - first) * ii
                imag = first * ii + (1.0 - first) * (ri - ir)
            else:
                real, imag = rr + ii, ri - ir
            for value, j in ((real, i), (imag, 8 + i)):
                base = pl.ds(pl.multiple_of((t * 16 + j) * PITCH, 8), 192)
                gram_a[base, :] = value[:, :128]
                gram_b[base, :64] = value[:, 128:]

    def step(s, _):
        @pl.when(s < PARTS)
        def _():
            start((0, 1, 3, 15, 16, 18, 7), s)

        @pl.when((s >= 1) & (s < PARTS + 1))
        def _():
            wait_in((0, 15), s - 1)
            start((2, 4, 17, 19, 8), s - 1)

        @pl.when((s >= 2) & (s < PARTS + 2))
        def _():
            wait_in((1, 4, 16, 19), s - 2)
            start((5, 6, 20, 21, 9, 12), s - 2)
            wait_in((2, 3), s - 2)
            start((10, 11), s - 2)

        @pl.when((s >= 3) & (s < PARTS + 3))
        def _():
            wait_in((5, 6), s - 3)
            start((13, 14), s - 3)

        @pl.when(s >= 4)
        def _():
            wait_in((17, 18, 20, 21, 7, 8, 9, 10, 11, 12, 13, 14), s - 4)
            score_part(s - 4)

        return 0

    lax.fori_loop(0, PARTS + 4, step, 0)

    scale_lead = jnp.sqrt(jnp.sum(e_lead[...], -1, keepdims=True) / (NX * NX * ENTRIES) + epsilon)
    ones = jnp.ones((8, 128), f32)
    across = lax.dot_general(ones, e_col[...], NT, precision=lax.Precision.HIGHEST, preferred_element_type=f32)
    scale_col = jnp.sqrt(across[:1] / (NX * NX * ENTRIES) + epsilon)
    e_lead[...] = jnp.broadcast_to(scale_lead, (96, 128))
    to_shift = shift[...]

    def best(b, _):
        found = []
        for u in range(8):
            a = b * 8 + u
            values = []
            for start_row in (a, a + 96):
                values.append(gram_a[pl.ds(start_row, NX, stride=PITCH), :])
                values.append(gram_b[pl.ds(start_row, NX, stride=PITCH), :][:, :64])
            value = jnp.concatenate(values, 1)
            high = value.astype(bf16)
            low = (value - high.astype(f32)).astype(bf16)
            moved = jnp.dot(to_shift, jnp.concatenate([high, low], 0), preferred_element_type=f32)
            top = jnp.max(moved[:NX] + moved[NX:], axis=0, keepdims=True)
            found.append(jnp.maximum(top[:, :192], top[:, 192:]))
        rows = pl.ds(pl.multiple_of(b * 8, 8), 8)
        scale = e_lead[rows, :]
        scale = jnp.concatenate([scale, scale[:, :64]], 1)
        out[rows, :] = jnp.concatenate(found, 0) / (math.sqrt(NX * ENTRIES) * scale * scale_col)
        return 0

    lax.fori_loop(0, 96 // 8, best, 0)

    def finish(t, _):
        for flow, (ref, slot, device) in sends.items():
            copy(flow, ref, slot, t, device).wait_send()
        return 0

    lax.fori_loop(0, PARTS, finish, 0)
    for e, device in enumerate(others):
        tell(e, my_row, device).wait_send()
        hand(e, device[0], my_row, device).wait_send()


def scores_of(count, slots, crossings):
    vmem = pl.BlockSpec(memory_space=pltpu.VMEM)
    smem = pl.BlockSpec(memory_space=pltpu.SMEM)
    return pl.pallas_call(
        score_kernel,
        out_shape=jax.ShapeDtypeStruct((COLS * M, ROWS * M), f32),
        in_specs=[smem, smem, pl.BlockSpec(memory_space=pl.ANY)] + [vmem] * 4,
        out_specs=vmem,
        scratch_shapes=[
            pltpu.VMEM((BUCKETS * ROWS, ENTRIES, NX), bf16),
            pltpu.VMEM((ROWS, BUCKETS, ENTRIES, NX), bf16),
            pltpu.VMEM((ROWS, BUCKETS, ENTRIES, NX), bf16),
            pltpu.VMEM((ROWS, 8, 128), jnp.int32),
            pltpu.SMEM((ROWS, 8, 128), jnp.int32),
            pltpu.SMEM((M,), jnp.int32),
            pltpu.VMEM((ROWS, M, NX, ENTRIES), bf16),
            pltpu.VMEM((COLS, M, NX, ENTRIES), bf16),
            pltpu.VMEM((16, 192, ENTRIES), bf16),
            pltpu.VMEM((16, 192, ENTRIES), bf16),
            pltpu.VMEM((NX * PITCH, 128), f32),
            pltpu.VMEM((NX * PITCH, 128), f32),
            pltpu.VMEM((96, 128), f32),
            pltpu.VMEM((192, 128), f32),
            pltpu.SemaphoreType.DMA,
            pltpu.SemaphoreType.DMA,
            pltpu.SemaphoreType.DMA((22, PARTS)),
            pltpu.SemaphoreType.DMA((22, PARTS)),
            pltpu.SemaphoreType.DMA((15,)),
            pltpu.SemaphoreType.DMA((15,)),
            pltpu.SemaphoreType.DMA((15,)),
            pltpu.SemaphoreType.DMA((15,)),
        ],
        compiler_params=pltpu.CompilerParams(
            collective_id=1, has_side_effects=True, vmem_limit_bytes=60 * 2**20
        ),
        name="scores",
    )(count, slots, crossings, *[jnp.asarray(table) for table in tables()])


def body(crossings, counts, dest):
    slot_total = crossings.shape[0]
    slot_ids = jnp.arange(slot_total, dtype=jnp.int32)
    slots = jnp.sum(jnp.where(dest.reshape(1, -1) == slot_ids[:, None], slot_ids[None, :], 0), 1)
    return scores_of(counts, slots, crossings.reshape(slot_total, ENTRIES, NX))


def solution(mesh):
    return jax.shard_map(
        body,
        mesh=mesh,
        in_specs=(P(("row", "col"), None, None, None), P("col", "row"), P(("row", "col"), None)),
        out_specs=P("row", "col"),
        check_vma=False,
    )
```

```python
import math

import jax
import jax.numpy as jnp
import ml_dtypes
import numpy as np
from jax import lax
from jax.experimental import pallas as pl
from jax.experimental.pallas import tpu as pltpu
from jax.sharding import PartitionSpec as P

M = 12
NX = 128
ENTRIES = 256
ROWS = 16
COLS = 8
BUCKETS = 3
PARTS = 8
PITCH_A = 200
PITCH_B = 104
AHEAD = 2

epsilon = 1e-06

MESH = pl.DeviceIdType.MESH
NT = (((1,), (1,)), ((), ()))
f32 = jnp.float32
bf16 = jnp.bfloat16


def split3(table):
    high = table.astype(ml_dtypes.bfloat16)
    rest = table - high.astype(np.float64)
    mid = rest.astype(ml_dtypes.bfloat16)
    low = (rest - mid.astype(np.float64)).astype(ml_dtypes.bfloat16)
    return high, mid, low


def tables():
    rows = np.arange(NX)
    part, inner = rows // 16, rows % 16
    wave = part * 8 + inner % 8
    imaginary = (inner >= 8) & (wave > 0)
    wave = np.where((inner >= 8) & (wave == 0), NX // 2, wave)
    points = np.arange(NX)
    angles = 2.0 * math.pi * ((wave[:, None] * points[None, :]) % NX) / NX
    forward = np.where(imaginary[:, None], -np.sin(angles), np.cos(angles))
    weight = np.where((wave == 0) | (wave == NX // 2), 1.0, 2.0)[:, None]
    inverse = weight * np.where(imaginary[:, None], -np.sin(angles), np.cos(angles)) / NX
    inverse = inverse - inverse.mean(1, keepdims=True)
    f_high, f_mid, f_low = split3(forward)
    forward_stack = np.concatenate([f_high, f_mid, f_low], 0)
    i_high, i_mid, _ = split3(inverse.T)
    shift = np.block([[i_high, i_high], [i_mid, np.zeros_like(i_mid)]])
    swap = np.zeros((256, 256))
    for first in range(16):
        for second in range(16):
            swap[first * 16 + second, second * 16 + first] = 1.0
    mirror = np.zeros((ENTRIES, ENTRIES))
    for point in range(128):
        mirror[(-point) % 128, point] = 1.0
        mirror[128 + (-point) % 128, 128 + point] = -1.0
    return (
        forward_stack.astype(ml_dtypes.bfloat16),
        swap.astype(ml_dtypes.bfloat16),
        mirror.astype(ml_dtypes.bfloat16),
        shift.astype(ml_dtypes.bfloat16),
    )


def dot_nt(a, b):
    return lax.dot_general(a, b, NT, preferred_element_type=f32)


def place():
    r = lax.axis_index("row")
    c = lax.axis_index("col")
    return r // 8, (r // 2) % 4, r % 2, c // 2, c % 2


OTHERS = [
    (1, 2, 0), (0, 1, 0), (0, 3, 0), (1, 0, 0), (0, 2, 0), (1, 1, 1), (1, 3, 1), (1, 2, 1), (0, 1, 1), (0, 3, 1),
    (1, 0, 1), (0, 2, 1), (1, 1, 0), (1, 3, 0), (0, 0, 1),
]


def score_kernel(
    count, dest, crossings, forward, swap, mirror, shift, out,
    held, staged, planes, tally, slots, picks, cols, leads, y_lead, y_col, gram_a, gram_b, e_lead, e_col,
    load, send, recv, hand_out, hand_in, count_out, count_in,
):
    fetch = pltpu.make_async_copy(crossings, held, load)
    fetch.start()
    z, x, k, y, h = place()
    my_row = z * 8 + x * 2 + k
    my_col = y * 2 + h

    def row_at(dz, dx, dk=0):
        return ((z + dz) % 2) * 8 + ((x + dx) % 4) * 2 + (k + dk) % 2

    def col_at(dh, dy):
        return ((y + dy) % 4) * 2 + (h + dh) % 2

    sib, zl = (row_at(0, 0, 1), my_col), (row_at(1, 0), my_col)
    xp, xm = (row_at(0, 1), my_col), (row_at(0, 3), my_col)
    zh, yp, ym = (my_row, col_at(1, 0)), (my_row, col_at(0, 1)), (my_row, col_at(0, 3))

    barrier = pltpu.get_barrier_semaphore()
    others = [(row_at(*step), my_col) for step in OTHERS]
    for device in others + [zh, yp, ym]:
        pl.semaphore_signal(barrier, inc=1, device_id=device, device_id_type=MESH)
    tally[my_row, 0] = count[0, 0]
    pl.semaphore_wait(barrier, len(OTHERS) + 3)

    def tell(e, row, device):
        return pltpu.make_async_remote_copy(
            src_ref=tally.at[row],
            dst_ref=tally.at[row],
            send_sem=count_out.at[e],
            recv_sem=count_in.at[e],
            device_id=device,
            device_id_type=MESH,
        )

    def hand(e, row, source, device):
        return pltpu.make_async_remote_copy(
            src_ref=staged.at[row],
            dst_ref=planes.at[source],
            send_sem=hand_out.at[e],
            recv_sem=hand_in.at[e],
            device_id=device,
            device_id_type=MESH,
        )

    senders = [row_at(dz, -dx, dk) for dz, dx, dk in OTHERS]
    for e, device in enumerate(others):
        tell(e, my_row, device).start()

    def find(n, _):
        slot = jnp.int32(0)
        for s in range(BUCKETS * ROWS):
            slot = jnp.where(dest[0, s] == n, s, slot)
        slots[n] = slot
        return 0

    lax.fori_loop(0, BUCKETS * ROWS, find, 0)
    for e, device in enumerate(others):
        tell(e, senders[e], device).wait_recv()
    fetch.wait()
    my_offset = jnp.int32(0)
    for r in range(ROWS):
        my_offset = my_offset + jnp.where(r < my_row, tally[r, 0], 0)

    for e, device in enumerate(others):
        target = device[0]
        for t in range(BUCKETS):
            staged[target, t] = held[slots[t * ROWS + (target + 256 * ROWS - my_offset) % ROWS]]
        hand(e, target, my_row, device).start()
    for t in range(BUCKETS):
        planes[my_row, t] = held[slots[t * ROWS + (my_row + 256 * ROWS - my_offset) % ROWS]]

    def pick(p, _):
        wanted = p * ROWS + my_row
        offset, found = jnp.int32(0), jnp.int32(0)
        for r in range(ROWS):
            within = wanted - offset
            hit = (within >= 0) & (within < tally[r, 0])
            found = jnp.where(hit, r * BUCKETS + within // ROWS, found)
            offset = offset + tally[r, 0]
        picks[p] = found
        return 0

    lax.fori_loop(0, M, pick, 0)
    for e, device in enumerate(others):
        hand(e, others[e][0], senders[e], device).wait_recv()

    def transform(b, _):
        for u in range(3):
            p = b * 3 + u
            source = picks[p]
            parts = dot_nt(forward[...], planes[source // BUCKETS, source % BUCKETS])
            value = (parts[:NX] + (parts[NX : 2 * NX] + parts[2 * NX :])).astype(bf16)
            for t in range(PARTS):
                cols[my_row, t, p] = value[t * 16 : (t + 1) * 16]
                leads[my_col, t, p] = value[t * 16 : (t + 1) * 16]
        return 0

    lax.fori_loop(0, M // 3, transform, 0)

    def piece(ref, slot, t):
        return ref.at[slot, t]

    def copy(flow, ref, slot, t, device):
        block = piece(ref, slot, t)
        return pltpu.make_async_remote_copy(
            src_ref=block,
            dst_ref=block,
            send_sem=send.at[flow, t],
            recv_sem=recv.at[flow, t],
            device_id=device,
            device_id_type=MESH,
        )

    own_c, own_l = row_at(0, 0), col_at(0, 0)
    sends = {
        0: (cols, own_c, zl), 1: (cols, own_c, xp), 3: (cols, own_c, xm), 7: (cols, own_c, sib),
        2: (cols, row_at(1, 0), xp), 4: (cols, row_at(1, 0), xm), 8: (cols, row_at(1, 0), sib),
        5: (cols, row_at(0, 3), xp), 9: (cols, row_at(0, 3), sib), 10: (cols, row_at(1, 3), sib),
        11: (cols, row_at(0, 1), sib), 6: (cols, row_at(1, 1), xm), 12: (cols, row_at(1, 1), sib),
        13: (cols, row_at(0, 2), sib), 14: (cols, row_at(1, 2), sib),
        15: (leads, own_l, zh), 16: (leads, own_l, yp), 18: (leads, own_l, ym),
        17: (leads, col_at(1, 0), yp), 19: (leads, col_at(1, 0), ym),
        20: (leads, col_at(0, 3), yp), 21: (leads, col_at(1, 1), ym),
    }
    arrives = {
        0: row_at(1, 0), 1: row_at(0, 3), 2: row_at(1, 3), 3: row_at(0, 1), 4: row_at(1, 1),
        5: row_at(0, 2), 6: row_at(1, 2),
        7: row_at(0, 0, 1), 8: row_at(1, 0, 1), 9: row_at(0, 3, 1), 10: row_at(1, 3, 1),
        11: row_at(0, 1, 1), 12: row_at(1, 1, 1), 13: row_at(0, 2, 1), 14: row_at(1, 2, 1),
        15: col_at(1, 0), 16: col_at(0, 3), 17: col_at(1, 3), 18: col_at(0, 1), 19: col_at(1, 1),
        20: col_at(0, 2), 21: col_at(1, 2),
    }

    def start(flows, t):
        for flow in flows:
            ref, slot, device = sends[flow]
            copy(flow, ref, slot, t, device).start()

    def wait_in(flows, t):
        for flow in flows:
            ref, _, device = sends[flow]
            copy(flow, ref, arrives[flow], t, device).wait_recv()

    e_lead[...] = jnp.zeros_like(e_lead)
    e_col[...] = jnp.zeros_like(e_col)

    def score_part(t):
        order = swap[...]

        def relay(ref, groups, dst):
            for g in range(groups):
                block = jnp.concatenate([ref[b // M, t, b % M] for b in range(g * 16, (g + 1) * 16)], 0)
                turned = jnp.dot(order, block, preferred_element_type=f32).astype(bf16)
                dst[:, g * 16 : (g + 1) * 16, :] = turned.reshape(16, 16, ENTRIES)

        relay(leads, 6, y_lead)
        relay(cols, 12, y_col)
        first = jnp.where(t == 0, 1.0, 0.0).astype(f32)
        for dst, source, count in ((e_lead, y_lead, 96), (e_col, y_col, 192)):
            total = dst[...]
            for j in range(16):
                value = source[j, :count, :].astype(f32)
                square = value * value
                square = square[:, :128] + square[:, 128:]
                weight = (2.0 - first) if j % 8 == 0 else 2.0
                total = total + weight * square
            dst[...] = total
        turn = mirror[...]
        for j in range(16):
            y_lead[j, 96:, :] = jnp.dot(y_lead[j, :96, :], turn, preferred_element_type=f32).astype(bf16)
        for i in range(8):
            lr, li, tr, ti = y_lead[i], y_lead[8 + i], y_col[i], y_col[8 + i]
            rr, ii, ri, ir = dot_nt(lr, tr), dot_nt(li, ti), dot_nt(lr, ti), dot_nt(li, tr)
            if i == 0:
                real = rr + (1.0 - first) * ii
                imag = first * ii + (1.0 - first) * (ri - ir)
            else:
                real, imag = rr + ii, ri - ir
            for value, j in ((real, i), (imag, 8 + i)):
                gram_a[pl.ds(pl.multiple_of((t * 16 + j) * PITCH_A, 8), 192), :] = value[:, :128]
                pair = jnp.concatenate([value[:96, 128:], value[96:, 128:]], 1)
                gram_b[pl.ds(pl.multiple_of((t * 16 + j) * PITCH_B, 8), 96), :] = pair

    own = (0, 15, 1, 3, 16, 18, 7)
    for t in range(AHEAD):
        start(own, t)

    def step(s, _):
        @pl.when(s < PARTS - AHEAD)
        def _():
            start(own, s + AHEAD)

        @pl.when(s < PARTS)
        def _():
            wait_in((0, 15), s)
            start((2, 4, 17, 19, 8), s)

        @pl.when((s >= 1) & (s < PARTS + 1))
        def _():
            wait_in((1, 16), s - 1)
            start((5, 20, 9), s - 1)
            wait_in((4, 19), s - 1)
            start((6, 21, 12), s - 1)
            wait_in((2, 3), s - 1)
            start((10, 11), s - 1)

        @pl.when((s >= 2) & (s < PARTS + 2))
        def _():
            wait_in((5, 6), s - 2)
            start((13, 14), s - 2)

        @pl.when(s >= 3)
        def _():
            wait_in((17, 18, 20, 21, 7, 8, 9, 10, 11, 12, 13, 14), s - 3)
            score_part(s - 3)
            for flow, (ref, slot, device) in sends.items():
                copy(flow, ref, slot, s - 3, device).wait_send()

        return 0

    lax.fori_loop(0, PARTS + 3, step, 0)

    scale_lead = jnp.sqrt(jnp.sum(e_lead[...], -1, keepdims=True) / (NX * NX * ENTRIES) + epsilon)
    ones = jnp.ones((8, 128), f32)
    across = lax.dot_general(ones, e_col[...], NT, precision=lax.Precision.HIGHEST, preferred_element_type=f32)
    scale_col = jnp.sqrt(across[:1] / (NX * NX * ENTRIES) + epsilon)
    e_lead[...] = jnp.broadcast_to(scale_lead, (96, 128))
    to_shift = shift[...]

    def best(b, _):
        found = []
        for u in range(0, 8, 2):
            values = []
            for a in (b * 8 + u, b * 8 + u + 1):
                values.append(gram_a[pl.ds(a, NX, stride=PITCH_A), :])
                values.append(gram_a[pl.ds(a + 96, NX, stride=PITCH_A), :])
                values.append(gram_b[pl.ds(a, NX, stride=PITCH_B), :])
            value = jnp.concatenate(values, 1)
            high = value.astype(bf16)
            low = (value - high.astype(f32)).astype(bf16)
            moved = jnp.dot(to_shift, jnp.concatenate([high, low], 0), preferred_element_type=f32)
            top = jnp.max(moved[:NX] + moved[NX:], axis=0, keepdims=True)
            found.extend([top[:, :384], top[:, 384:]])
        found = jnp.concatenate(found, 0)
        found = jnp.concatenate(
            [jnp.maximum(found[:, :128], found[:, 128:256]), jnp.maximum(found[:, 256:320], found[:, 320:])], 1
        )
        rows = pl.ds(pl.multiple_of(b * 8, 8), 8)
        scale = e_lead[rows, :]
        scale = jnp.concatenate([scale, scale[:, :64]], 1)
        out[rows, :] = found / (math.sqrt(NX * ENTRIES) * scale * scale_col)
        return 0

    lax.fori_loop(0, 96 // 8, best, 0)

    for e, device in enumerate(others):
        tell(e, my_row, device).wait_send()
        hand(e, device[0], my_row, device).wait_send()


def scores_of(count, dest, crossings):
    vmem = pl.BlockSpec(memory_space=pltpu.VMEM)
    smem = pl.BlockSpec(memory_space=pltpu.SMEM)
    return pl.pallas_call(
        score_kernel,
        out_shape=jax.ShapeDtypeStruct((COLS * M, ROWS * M), f32),
        in_specs=[smem, smem, pl.BlockSpec(memory_space=pl.ANY)] + [vmem] * 4,
        out_specs=vmem,
        scratch_shapes=[
            pltpu.VMEM((BUCKETS * ROWS, ENTRIES, NX), bf16),
            pltpu.VMEM((ROWS, BUCKETS, ENTRIES, NX), bf16),
            pltpu.VMEM((ROWS, BUCKETS, ENTRIES, NX), bf16),
            pltpu.SMEM((ROWS, 128), jnp.int32),
            pltpu.SMEM((BUCKETS * ROWS,), jnp.int32),
            pltpu.SMEM((M,), jnp.int32),
            pltpu.VMEM((ROWS, PARTS, M, 16, ENTRIES), bf16),
            pltpu.VMEM((COLS, PARTS, M, 16, ENTRIES), bf16),
            pltpu.VMEM((16, 192, ENTRIES), bf16),
            pltpu.VMEM((16, 192, ENTRIES), bf16),
            pltpu.VMEM((NX * PITCH_A, 128), f32),
            pltpu.VMEM((NX * PITCH_B, 128), f32),
            pltpu.VMEM((96, 128), f32),
            pltpu.VMEM((192, 128), f32),
            pltpu.SemaphoreType.DMA,
            pltpu.SemaphoreType.DMA((22, PARTS)),
            pltpu.SemaphoreType.DMA((22, PARTS)),
            pltpu.SemaphoreType.DMA((15,)),
            pltpu.SemaphoreType.DMA((15,)),
            pltpu.SemaphoreType.DMA((15,)),
            pltpu.SemaphoreType.DMA((15,)),
        ],
        compiler_params=pltpu.CompilerParams(
            collective_id=1, has_side_effects=True, vmem_limit_bytes=60 * 2**20
        ),
        name="scores",
    )(count, dest, crossings, *[jnp.asarray(table) for table in tables()])


def body(crossings, counts, dest):
    return scores_of(counts, dest, crossings.reshape(BUCKETS * ROWS, ENTRIES, NX))


def solution(mesh):
    return jax.shard_map(
        body,
        mesh=mesh,
        in_specs=(P(("row", "col"), None, None, None), P("col", "row"), P(("row", "col"), None)),
        out_specs=P("row", "col"),
        check_vma=False,
    )
```

```python
import math

import jax
import jax.numpy as jnp
import ml_dtypes
import numpy as np
from jax import lax
from jax.experimental import pallas as pl
from jax.experimental.pallas import tpu as pltpu
from jax.sharding import PartitionSpec as P

M = 12
NX = 128
ENTRIES = 256
ROWS = 16
COLS = 8
BUCKETS = 3
PARTS = 8
PITCH_A = 200
PITCH_B = 104
GROUP = 2
GROUPS = PARTS // GROUP
EARLY = 2
AHEAD = 3

epsilon = 1e-06

MESH = pl.DeviceIdType.MESH
NT = (((1,), (1,)), ((), ()))
f32 = jnp.float32
bf16 = jnp.bfloat16


def split3(table):
    high = table.astype(ml_dtypes.bfloat16)
    rest = table - high.astype(np.float64)
    mid = rest.astype(ml_dtypes.bfloat16)
    low = (rest - mid.astype(np.float64)).astype(ml_dtypes.bfloat16)
    return high, mid, low


def tables():
    rows = np.arange(NX)
    part, inner = rows // 16, rows % 16
    wave = part * 8 + inner % 8
    imaginary = (inner >= 8) & (wave > 0)
    wave = np.where((inner >= 8) & (wave == 0), NX // 2, wave)
    points = np.arange(NX)
    angles = 2.0 * math.pi * ((wave[:, None] * points[None, :]) % NX) / NX
    forward = np.where(imaginary[:, None], -np.sin(angles), np.cos(angles))
    weight = np.where((wave == 0) | (wave == NX // 2), 1.0, 2.0)[:, None]
    inverse = weight * np.where(imaginary[:, None], -np.sin(angles), np.cos(angles)) / NX
    inverse = inverse - inverse.mean(1, keepdims=True)
    f_high, f_mid, f_low = split3(forward)
    forward_stack = np.concatenate([f_high, f_mid, f_low], 0)
    i_high, i_mid, _ = split3(inverse.T)
    shift = np.block([[i_high, i_high], [i_mid, np.zeros_like(i_mid)]])
    swap = np.zeros((256, 256))
    for first in range(16):
        for second in range(16):
            swap[first * 16 + second, second * 16 + first] = 1.0
    mirror = np.zeros((ENTRIES, ENTRIES))
    for point in range(128):
        mirror[(-point) % 128, point] = 1.0
        mirror[128 + (-point) % 128, 128 + point] = -1.0
    return (
        forward_stack.astype(ml_dtypes.bfloat16),
        swap.astype(ml_dtypes.bfloat16),
        mirror.astype(ml_dtypes.bfloat16),
        shift.astype(ml_dtypes.bfloat16),
    )


def dot_nt(a, b):
    return lax.dot_general(a, b, NT, preferred_element_type=f32)


def place():
    r = lax.axis_index("row")
    c = lax.axis_index("col")
    return r // 8, (r // 2) % 4, r % 2, c // 2, c % 2


OTHERS = [
    (1, 2, 0), (0, 1, 0), (0, 3, 0), (1, 0, 0), (0, 2, 0), (1, 1, 1), (1, 3, 1), (1, 2, 1), (0, 1, 1), (0, 3, 1),
    (1, 0, 1), (0, 2, 1), (1, 1, 0), (1, 3, 0), (0, 0, 1),
]


def score_kernel(
    count, dest, crossings, forward, swap, mirror, shift, out,
    held, coeffs, staged, planes_0, planes_1, planes_2, planes_3, tally, slots, picks, cols, leads, y_lead, y_col, gram_a, gram_b, e_lead, e_col,
    load, send, recv, hand_out, hand_in, count_out, count_in,
):
    fetch = pltpu.make_async_copy(crossings, held, load)
    fetch.start()
    z, x, k, y, h = place()
    my_row = z * 8 + x * 2 + k
    my_col = y * 2 + h

    def row_at(dz, dx, dk=0):
        return ((z + dz) % 2) * 8 + ((x + dx) % 4) * 2 + (k + dk) % 2

    def col_at(dh, dy):
        return ((y + dy) % 4) * 2 + (h + dh) % 2

    sib, zl = (row_at(0, 0, 1), my_col), (row_at(1, 0), my_col)
    xp, xm = (row_at(0, 1), my_col), (row_at(0, 3), my_col)
    zh, yp, ym = (my_row, col_at(1, 0)), (my_row, col_at(0, 1)), (my_row, col_at(0, 3))

    barrier = pltpu.get_barrier_semaphore()
    others = [(row_at(*step), my_col) for step in OTHERS]
    for device in others + [zh, yp, ym]:
        pl.semaphore_signal(barrier, inc=1, device_id=device, device_id_type=MESH)
    tally[my_row, 0] = count[0, 0]
    pl.semaphore_wait(barrier, len(OTHERS) + 3)

    def tell(e, row, device):
        return pltpu.make_async_remote_copy(
            src_ref=tally.at[row],
            dst_ref=tally.at[row],
            send_sem=count_out.at[e],
            recv_sem=count_in.at[e],
            device_id=device,
            device_id_type=MESH,
        )

    planes = (planes_0, planes_1, planes_2, planes_3)

    def hand(e, group, row, source, device):
        return pltpu.make_async_remote_copy(
            src_ref=staged.at[row, group],
            dst_ref=planes[group].at[source],
            send_sem=hand_out.at[e, group],
            recv_sem=hand_in.at[e, group],
            device_id=device,
            device_id_type=MESH,
        )

    senders = [row_at(dz, -dx, dk) for dz, dx, dk in OTHERS]
    for e, device in enumerate(others):
        tell(e, my_row, device).start()
    fetch.wait()

    def prepare(b, _):
        for u in range(4):
            n = b * 4 + u
            slot = jnp.int32(0)
            for s in range(BUCKETS * ROWS):
                slot = jnp.where(dest[0, s] == n, s, slot)
            slots[n] = slot
            parts = dot_nt(forward[...], held[n])
            value = (parts[:NX] + (parts[NX : 2 * NX] + parts[2 * NX :])).astype(bf16)
            for t in range(PARTS):
                coeffs[n, t] = value[t * 16 : (t + 1) * 16]
        return 0

    lax.fori_loop(0, BUCKETS * ROWS // 4, prepare, 0)
    for e, device in enumerate(others):
        tell(e, senders[e], device).wait_recv()
    my_offset = jnp.int32(0)
    for r in range(ROWS):
        my_offset = my_offset + jnp.where(r < my_row, tally[r, 0], 0)

    def hand_over(group):
        for e, device in enumerate(others):
            target = device[0]
            for t in range(BUCKETS):
                slot = slots[t * ROWS + (target + 256 * ROWS - my_offset) % ROWS]
                for g in range(GROUP):
                    staged[target, group, t, g] = coeffs[slot, group * GROUP + g]
            hand(e, group, target, my_row, device).start()
        for t in range(BUCKETS):
            slot = slots[t * ROWS + (my_row + 256 * ROWS - my_offset) % ROWS]
            for g in range(GROUP):
                planes[group][my_row, t, g] = coeffs[slot, group * GROUP + g]

    def take(group):
        for e, device in enumerate(others):
            hand(e, group, device[0], senders[e], device).wait_recv()
        for p in range(M):
            source = picks[p]
            for g in range(GROUP):
                value = planes[group][source // BUCKETS, source % BUCKETS, g]
                cols[my_row, group * GROUP + g, p] = value
                leads[my_col, group * GROUP + g, p] = value

    for group in range(EARLY):
        hand_over(group)

    def pick(p, _):
        wanted = p * ROWS + my_row
        offset, found = jnp.int32(0), jnp.int32(0)
        for r in range(ROWS):
            within = wanted - offset
            hit = (within >= 0) & (within < tally[r, 0])
            found = jnp.where(hit, r * BUCKETS + within // ROWS, found)
            offset = offset + tally[r, 0]
        picks[p] = found
        return 0

    lax.fori_loop(0, M, pick, 0)

    def piece(ref, slot, t):
        return ref.at[slot, t]

    def copy(flow, ref, slot, t, device):
        block = piece(ref, slot, t)
        return pltpu.make_async_remote_copy(
            src_ref=block,
            dst_ref=block,
            send_sem=send.at[flow, t],
            recv_sem=recv.at[flow, t],
            device_id=device,
            device_id_type=MESH,
        )

    own_c, own_l = row_at(0, 0), col_at(0, 0)
    sends = {
        0: (cols, own_c, zl), 1: (cols, own_c, xp), 3: (cols, own_c, xm), 7: (cols, own_c, sib),
        2: (cols, row_at(1, 0), xp), 4: (cols, row_at(1, 0), xm), 8: (cols, row_at(1, 0), sib),
        5: (cols, row_at(0, 3), xp), 9: (cols, row_at(0, 3), sib), 10: (cols, row_at(1, 3), sib),
        11: (cols, row_at(0, 1), sib), 6: (cols, row_at(1, 1), xm), 12: (cols, row_at(1, 1), sib),
        13: (cols, row_at(0, 2), sib), 14: (cols, row_at(1, 2), sib),
        15: (leads, own_l, zh), 16: (leads, own_l, yp), 18: (leads, own_l, ym),
        17: (leads, col_at(1, 0), yp), 19: (leads, col_at(1, 0), ym),
        20: (leads, col_at(0, 3), yp), 21: (leads, col_at(1, 1), ym),
    }
    arrives = {
        0: row_at(1, 0), 1: row_at(0, 3), 2: row_at(1, 3), 3: row_at(0, 1), 4: row_at(1, 1),
        5: row_at(0, 2), 6: row_at(1, 2),
        7: row_at(0, 0, 1), 8: row_at(1, 0, 1), 9: row_at(0, 3, 1), 10: row_at(1, 3, 1),
        11: row_at(0, 1, 1), 12: row_at(1, 1, 1), 13: row_at(0, 2, 1), 14: row_at(1, 2, 1),
        15: col_at(1, 0), 16: col_at(0, 3), 17: col_at(1, 3), 18: col_at(0, 1), 19: col_at(1, 1),
        20: col_at(0, 2), 21: col_at(1, 2),
    }

    def start(flows, t):
        for flow in flows:
            ref, slot, device = sends[flow]
            copy(flow, ref, slot, t, device).start()

    def wait_in(flows, t):
        for flow in flows:
            ref, _, device = sends[flow]
            copy(flow, ref, arrives[flow], t, device).wait_recv()

    e_lead[...] = jnp.zeros_like(e_lead)
    e_col[...] = jnp.zeros_like(e_col)

    def score_part(t):
        order = swap[...]

        def relay(ref, groups, dst):
            for g in range(groups):
                block = jnp.concatenate([ref[b // M, t, b % M] for b in range(g * 16, (g + 1) * 16)], 0)
                turned = jnp.dot(order, block, preferred_element_type=f32).astype(bf16)
                dst[:, g * 16 : (g + 1) * 16, :] = turned.reshape(16, 16, ENTRIES)

        relay(leads, 6, y_lead)
        relay(cols, 12, y_col)
        first = jnp.where(t == 0, 1.0, 0.0).astype(f32)
        for dst, source, count in ((e_lead, y_lead, 96), (e_col, y_col, 192)):
            total = dst[...]
            for j in range(16):
                value = source[j, :count, :].astype(f32)
                square = value * value
                square = square[:, :128] + square[:, 128:]
                weight = (2.0 - first) if j % 8 == 0 else 2.0
                total = total + weight * square
            dst[...] = total
        turn = mirror[...]
        for j in range(16):
            y_lead[j, 96:, :] = jnp.dot(y_lead[j, :96, :], turn, preferred_element_type=f32).astype(bf16)
        for i in range(8):
            lr, li, tr, ti = y_lead[i], y_lead[8 + i], y_col[i], y_col[8 + i]
            rr, ii, ri, ir = dot_nt(lr, tr), dot_nt(li, ti), dot_nt(lr, ti), dot_nt(li, tr)
            if i == 0:
                real = rr + (1.0 - first) * ii
                imag = first * ii + (1.0 - first) * (ri - ir)
            else:
                real, imag = rr + ii, ri - ir
            for value, j in ((real, i), (imag, 8 + i)):
                gram_a[pl.ds(pl.multiple_of((t * 16 + j) * PITCH_A, 8), 192), :] = value[:, :128]
                pair = jnp.concatenate([value[:96, 128:], value[96:, 128:]], 1)
                gram_b[pl.ds(pl.multiple_of((t * 16 + j) * PITCH_B, 8), 96), :] = pair

    def step(s, _):
        for group in range(GROUPS):
            @pl.when(s == group * GROUP)
            def _():
                take(group)
                if group + EARLY < GROUPS:
                    hand_over(group + EARLY)

        @pl.when(s < PARTS)
        def _():
            start((0, 15, 1, 3, 16, 18, 7), s)

        @pl.when((s >= AHEAD) & (s < PARTS + AHEAD))
        def _():
            wait_in((0, 15), s - AHEAD)
            start((2, 4, 17, 19, 8), s - AHEAD)

        @pl.when((s >= AHEAD + 1) & (s < PARTS + AHEAD + 1))
        def _():
            t = s - AHEAD - 1
            wait_in((1, 16), t)
            start((5, 20, 9), t)
            wait_in((4, 19), t)
            start((6, 21, 12), t)
            wait_in((2, 3), t)
            start((10, 11), t)

        @pl.when((s >= AHEAD + 2) & (s < PARTS + AHEAD + 2))
        def _():
            wait_in((5, 6), s - AHEAD - 2)
            start((13, 14), s - AHEAD - 2)

        @pl.when(s >= AHEAD + 3)
        def _():
            t = s - AHEAD - 3
            wait_in((17, 18, 20, 21, 7, 8, 9, 10, 11, 12, 13, 14), t)
            score_part(t)
            for flow, (ref, slot, device) in sends.items():
                copy(flow, ref, slot, t, device).wait_send()

        return 0

    lax.fori_loop(0, PARTS + AHEAD + 3, step, 0)

    scale_lead = jnp.sqrt(jnp.sum(e_lead[...], -1, keepdims=True) / (NX * NX * ENTRIES) + epsilon)
    ones = jnp.ones((8, 128), f32)
    across = lax.dot_general(ones, e_col[...], NT, precision=lax.Precision.HIGHEST, preferred_element_type=f32)
    scale_col = jnp.sqrt(across[:1] / (NX * NX * ENTRIES) + epsilon)
    e_lead[...] = jnp.broadcast_to(scale_lead, (96, 128))
    to_shift = shift[...]

    def best(b, _):
        found = []
        for u in range(0, 8, 2):
            values = []
            for a in (b * 8 + u, b * 8 + u + 1):
                values.append(gram_a[pl.ds(a, NX, stride=PITCH_A), :])
                values.append(gram_a[pl.ds(a + 96, NX, stride=PITCH_A), :])
                values.append(gram_b[pl.ds(a, NX, stride=PITCH_B), :])
            value = jnp.concatenate(values, 1)
            high = value.astype(bf16)
            low = (value - high.astype(f32)).astype(bf16)
            moved = jnp.dot(to_shift, jnp.concatenate([high, low], 0), preferred_element_type=f32)
            top = jnp.max(moved[:NX] + moved[NX:], axis=0, keepdims=True)
            found.extend([top[:, :384], top[:, 384:]])
        found = jnp.concatenate(found, 0)
        found = jnp.concatenate(
            [jnp.maximum(found[:, :128], found[:, 128:256]), jnp.maximum(found[:, 256:320], found[:, 320:])], 1
        )
        rows = pl.ds(pl.multiple_of(b * 8, 8), 8)
        scale = e_lead[rows, :]
        scale = jnp.concatenate([scale, scale[:, :64]], 1)
        out[rows, :] = found / (math.sqrt(NX * ENTRIES) * scale * scale_col)
        return 0

    lax.fori_loop(0, 96 // 8, best, 0)

    for e, device in enumerate(others):
        tell(e, my_row, device).wait_send()
        for group in range(GROUPS):
            hand(e, group, device[0], my_row, device).wait_send()


def scores_of(count, dest, crossings):
    vmem = pl.BlockSpec(memory_space=pltpu.VMEM)
    smem = pl.BlockSpec(memory_space=pltpu.SMEM)
    return pl.pallas_call(
        score_kernel,
        out_shape=jax.ShapeDtypeStruct((COLS * M, ROWS * M), f32),
        in_specs=[smem, smem, pl.BlockSpec(memory_space=pl.ANY)] + [vmem] * 4,
        out_specs=vmem,
        scratch_shapes=[
            pltpu.VMEM((BUCKETS * ROWS, ENTRIES, NX), bf16),
            pltpu.VMEM((BUCKETS * ROWS, PARTS, 16, ENTRIES), bf16),
            pltpu.VMEM((ROWS, GROUPS, BUCKETS, GROUP, 16, ENTRIES), bf16),
            *[pltpu.VMEM((ROWS, BUCKETS, GROUP, 16, ENTRIES), bf16)] * GROUPS,
            pltpu.SMEM((ROWS, 128), jnp.int32),
            pltpu.SMEM((BUCKETS * ROWS,), jnp.int32),
            pltpu.SMEM((M,), jnp.int32),
            pltpu.VMEM((ROWS, PARTS, M, 16, ENTRIES), bf16),
            pltpu.VMEM((COLS, PARTS, M, 16, ENTRIES), bf16),
            pltpu.VMEM((16, 192, ENTRIES), bf16),
            pltpu.VMEM((16, 192, ENTRIES), bf16),
            pltpu.VMEM((NX * PITCH_A, 128), f32),
            pltpu.VMEM((NX * PITCH_B, 128), f32),
            pltpu.VMEM((96, 128), f32),
            pltpu.VMEM((192, 128), f32),
            pltpu.SemaphoreType.DMA,
            pltpu.SemaphoreType.DMA((22, PARTS)),
            pltpu.SemaphoreType.DMA((22, PARTS)),
            pltpu.SemaphoreType.DMA((15, GROUPS)),
            pltpu.SemaphoreType.DMA((15, GROUPS)),
            pltpu.SemaphoreType.DMA((15,)),
            pltpu.SemaphoreType.DMA((15,)),
        ],
        compiler_params=pltpu.CompilerParams(
            collective_id=1, has_side_effects=True, vmem_limit_bytes=60 * 2**20
        ),
        name="scores",
    )(count, dest, crossings, *[jnp.asarray(table) for table in tables()])


def body(crossings, counts, dest):
    return scores_of(counts, dest, crossings.reshape(BUCKETS * ROWS, ENTRIES, NX))


def solution(mesh):
    return jax.shard_map(
        body,
        mesh=mesh,
        in_specs=(P(("row", "col"), None, None, None), P("col", "row"), P(("row", "col"), None)),
        out_specs=P("row", "col"),
        check_vma=False,
    )
```

```python
import math

import jax
import jax.numpy as jnp
import ml_dtypes
import numpy as np
from jax import lax
from jax.experimental import pallas as pl
from jax.experimental.pallas import tpu as pltpu
from jax.sharding import PartitionSpec as P

M = 12
NX = 128
ENTRIES = 256
ROWS = 16
COLS = 8
BUCKETS = 3
PARTS = 8
PITCH_A = 200
PITCH_B = 104
GROUP = 2
GROUPS = PARTS // GROUP
EARLY = 2
AHEAD = 3

epsilon = 1e-06

MESH = pl.DeviceIdType.MESH
NT = (((1,), (1,)), ((), ()))
f32 = jnp.float32
bf16 = jnp.bfloat16


def split3(table):
    high = table.astype(ml_dtypes.bfloat16)
    rest = table - high.astype(np.float64)
    mid = rest.astype(ml_dtypes.bfloat16)
    low = (rest - mid.astype(np.float64)).astype(ml_dtypes.bfloat16)
    return high, mid, low


def tables():
    rows = np.arange(NX)
    part, inner = rows // 16, rows % 16
    wave = part * 8 + inner % 8
    imaginary = (inner >= 8) & (wave > 0)
    wave = np.where((inner >= 8) & (wave == 0), NX // 2, wave)
    points = np.arange(NX)
    angles = 2.0 * math.pi * ((wave[:, None] * points[None, :]) % NX) / NX
    forward = np.where(imaginary[:, None], -np.sin(angles), np.cos(angles))
    weight = np.where((wave == 0) | (wave == NX // 2), 1.0, 2.0)[:, None]
    inverse = weight * np.where(imaginary[:, None], -np.sin(angles), np.cos(angles)) / NX
    inverse = inverse - inverse.mean(1, keepdims=True)
    f_high, f_mid, f_low = split3(forward)
    forward_stack = np.concatenate([f_high, f_mid, f_low], 0)
    i_high, i_mid, _ = split3(inverse.T)
    shift = np.block([[i_high, i_high], [i_mid, np.zeros_like(i_mid)]])
    swap = np.zeros((256, 256))
    for first in range(16):
        for second in range(16):
            swap[first * 16 + second, second * 16 + first] = 1.0
    mirror = np.zeros((ENTRIES, ENTRIES))
    for point in range(128):
        mirror[(-point) % 128, point] = 1.0
        mirror[128 + (-point) % 128, 128 + point] = -1.0
    return (
        forward_stack.astype(ml_dtypes.bfloat16),
        swap.astype(ml_dtypes.bfloat16),
        mirror.astype(ml_dtypes.bfloat16),
        shift.astype(ml_dtypes.bfloat16),
    )


def dot_nt(a, b):
    return lax.dot_general(a, b, NT, preferred_element_type=f32)


def place():
    r = lax.axis_index("row")
    c = lax.axis_index("col")
    return r // 8, (r // 2) % 4, r % 2, c // 2, c % 2


OTHERS = [
    (1, 2, 0), (0, 1, 0), (0, 3, 0), (1, 0, 0), (0, 2, 0), (1, 1, 1), (1, 3, 1), (1, 2, 1), (0, 1, 1), (0, 3, 1),
    (1, 0, 1), (0, 2, 1), (1, 1, 0), (1, 3, 0), (0, 0, 1),
]


def score_kernel(
    count, dest, crossings, forward, swap, mirror, shift, out,
    held, coeffs, staged, planes_0, planes_1, planes_2, planes_3, tally, slots, picks, cols, leads, y_lead, y_col, gram_a, gram_b, e_lead, e_col,
    load, send, recv, hand_out, hand_in, count_out, count_in,
):
    fetch = pltpu.make_async_copy(crossings, held, load)
    fetch.start()
    z, x, k, y, h = place()
    my_row = z * 8 + x * 2 + k
    my_col = y * 2 + h

    def row_at(dz, dx, dk=0):
        return ((z + dz) % 2) * 8 + ((x + dx) % 4) * 2 + (k + dk) % 2

    def col_at(dh, dy):
        return ((y + dy) % 4) * 2 + (h + dh) % 2

    sib, zl = (row_at(0, 0, 1), my_col), (row_at(1, 0), my_col)
    xp, xm = (row_at(0, 1), my_col), (row_at(0, 3), my_col)
    zh, yp, ym = (my_row, col_at(1, 0)), (my_row, col_at(0, 1)), (my_row, col_at(0, 3))

    barrier = pltpu.get_barrier_semaphore()
    others = [(row_at(*step), my_col) for step in OTHERS]
    for device in others + [zh, yp, ym]:
        pl.semaphore_signal(barrier, inc=1, device_id=device, device_id_type=MESH)
    tally[my_row, 0] = count[0, 0]
    pl.semaphore_wait(barrier, len(OTHERS) + 3)

    def tell(e, row, device):
        return pltpu.make_async_remote_copy(
            src_ref=tally.at[row],
            dst_ref=tally.at[row],
            send_sem=count_out.at[e],
            recv_sem=count_in.at[e],
            device_id=device,
            device_id_type=MESH,
        )

    planes = (planes_0, planes_1, planes_2, planes_3)

    def hand(e, group, row, source, device):
        return pltpu.make_async_remote_copy(
            src_ref=staged.at[row, group],
            dst_ref=planes[group].at[source],
            send_sem=hand_out.at[e, group],
            recv_sem=hand_in.at[e, group],
            device_id=device,
            device_id_type=MESH,
        )

    senders = [row_at(dz, -dx, dk) for dz, dx, dk in OTHERS]
    for e, device in enumerate(others):
        tell(e, my_row, device).start()
    fetch.wait()

    def prepare(b, _):
        for u in range(4):
            n = b * 4 + u
            slot = jnp.int32(0)
            for s in range(BUCKETS * ROWS):
                slot = jnp.where(dest[0, s] == n, s, slot)
            slots[n] = slot
            parts = dot_nt(forward[...], held[n])
            value = (parts[:NX] + (parts[NX : 2 * NX] + parts[2 * NX :])).astype(bf16)
            for t in range(PARTS):
                coeffs[n, t] = value[t * 16 : (t + 1) * 16]
        return 0

    lax.fori_loop(0, BUCKETS * ROWS // 4, prepare, 0)
    for e, device in enumerate(others):
        tell(e, senders[e], device).wait_recv()
    my_offset = jnp.int32(0)
    for r in range(ROWS):
        my_offset = my_offset + jnp.where(r < my_row, tally[r, 0], 0)

    def hand_over(group):
        for e, device in enumerate(others):
            target = device[0]
            for t in range(BUCKETS):
                slot = slots[t * ROWS + (target + 256 * ROWS - my_offset) % ROWS]
                for g in range(GROUP):
                    staged[target, group, t, g] = coeffs[slot, group * GROUP + g]
            hand(e, group, target, my_row, device).start()
        for t in range(BUCKETS):
            slot = slots[t * ROWS + (my_row + 256 * ROWS - my_offset) % ROWS]
            for g in range(GROUP):
                planes[group][my_row, t, g] = coeffs[slot, group * GROUP + g]

    def take(group):
        for e, device in enumerate(others):
            hand(e, group, device[0], senders[e], device).wait_recv()
        for p in range(M):
            source = picks[p]
            for g in range(GROUP):
                value = planes[group][source // BUCKETS, source % BUCKETS, g]
                cols[my_row, group * GROUP + g, p] = value
                leads[my_col, group * GROUP + g, p] = value

    for group in range(EARLY):
        hand_over(group)

    def pick(p, _):
        wanted = p * ROWS + my_row
        offset, found = jnp.int32(0), jnp.int32(0)
        for r in range(ROWS):
            within = wanted - offset
            hit = (within >= 0) & (within < tally[r, 0])
            found = jnp.where(hit, r * BUCKETS + within // ROWS, found)
            offset = offset + tally[r, 0]
        picks[p] = found
        return 0

    lax.fori_loop(0, M, pick, 0)

    def piece(ref, slot, t):
        return ref.at[slot, t]

    def copy(flow, ref, slot, t, device):
        block = piece(ref, slot, t)
        return pltpu.make_async_remote_copy(
            src_ref=block,
            dst_ref=block,
            send_sem=send.at[flow, t],
            recv_sem=recv.at[flow, t],
            device_id=device,
            device_id_type=MESH,
        )

    own_c, own_l = row_at(0, 0), col_at(0, 0)
    sends = {
        0: (cols, own_c, zl), 1: (cols, own_c, xp), 3: (cols, own_c, xm), 7: (cols, own_c, sib),
        2: (cols, row_at(1, 0), xp), 4: (cols, row_at(1, 0), xm), 8: (cols, row_at(1, 0), sib),
        5: (cols, row_at(0, 3), xp), 9: (cols, row_at(0, 3), sib), 10: (cols, row_at(1, 3), sib),
        11: (cols, row_at(0, 1), sib), 6: (cols, row_at(1, 1), xm), 12: (cols, row_at(1, 1), sib),
        13: (cols, row_at(0, 2), sib), 14: (cols, row_at(1, 2), sib),
        15: (leads, own_l, zh), 16: (leads, own_l, yp), 18: (leads, own_l, ym),
        17: (leads, col_at(1, 0), yp), 19: (leads, col_at(1, 0), ym),
        20: (leads, col_at(0, 3), yp), 21: (leads, col_at(1, 1), ym),
    }
    arrives = {
        0: row_at(1, 0), 1: row_at(0, 3), 2: row_at(1, 3), 3: row_at(0, 1), 4: row_at(1, 1),
        5: row_at(0, 2), 6: row_at(1, 2),
        7: row_at(0, 0, 1), 8: row_at(1, 0, 1), 9: row_at(0, 3, 1), 10: row_at(1, 3, 1),
        11: row_at(0, 1, 1), 12: row_at(1, 1, 1), 13: row_at(0, 2, 1), 14: row_at(1, 2, 1),
        15: col_at(1, 0), 16: col_at(0, 3), 17: col_at(1, 3), 18: col_at(0, 1), 19: col_at(1, 1),
        20: col_at(0, 2), 21: col_at(1, 2),
    }

    def start(flows, t):
        for flow in flows:
            ref, slot, device = sends[flow]
            copy(flow, ref, slot, t, device).start()

    def wait_in(flows, t):
        for flow in flows:
            ref, _, device = sends[flow]
            copy(flow, ref, arrives[flow], t, device).wait_recv()

    e_lead[...] = jnp.zeros_like(e_lead)
    e_col[...] = jnp.zeros_like(e_col)

    def score_part(t):
        order = swap[...]

        def relay(ref, groups, dst):
            for g in range(groups):
                block = jnp.concatenate([ref[b // M, t, b % M] for b in range(g * 16, (g + 1) * 16)], 0)
                turned = jnp.dot(order, block, preferred_element_type=f32).astype(bf16)
                dst[:, g * 16 : (g + 1) * 16, :] = turned.reshape(16, 16, ENTRIES)

        relay(leads, 6, y_lead)
        relay(cols, 12, y_col)
        first = jnp.where(t == 0, 1.0, 0.0).astype(f32)
        for dst, source, count in ((e_lead, y_lead, 96), (e_col, y_col, 192)):
            total = dst[...]
            for j in range(16):
                value = source[j, :count, :].astype(f32)
                square = value * value
                square = square[:, :128] + square[:, 128:]
                weight = (2.0 - first) if j % 8 == 0 else 2.0
                total = total + weight * square
            dst[...] = total
        turn = mirror[...]
        for j in range(16):
            y_lead[j, 96:, :] = jnp.dot(y_lead[j, :96, :], turn, preferred_element_type=f32).astype(bf16)
        for i in range(8):
            lr, li, tr, ti = y_lead[i], y_lead[8 + i], y_col[i], y_col[8 + i]
            both = jnp.concatenate([lr, li], 0)
            with_real, with_imag = dot_nt(both, tr), dot_nt(both, ti)
            rr, ir, ri, ii = with_real[:192], with_real[192:], with_imag[:192], with_imag[192:]
            if i == 0:
                real = rr + (1.0 - first) * ii
                imag = first * ii + (1.0 - first) * (ri - ir)
            else:
                real, imag = rr + ii, ri - ir
            for value, j in ((real, i), (imag, 8 + i)):
                gram_a[pl.ds(pl.multiple_of((t * 16 + j) * PITCH_A, 8), 192), :] = value[:, :128]
                pair = jnp.concatenate([value[:96, 128:], value[96:, 128:]], 1)
                gram_b[pl.ds(pl.multiple_of((t * 16 + j) * PITCH_B, 8), 96), :] = pair

    def step(s, _):
        for group in range(GROUPS):
            @pl.when(s == group * GROUP)
            def _():
                take(group)
                if group + EARLY < GROUPS:
                    hand_over(group + EARLY)

        @pl.when(s < PARTS)
        def _():
            start((0, 15, 1, 3, 16, 18, 7), s)

        @pl.when((s >= AHEAD) & (s < PARTS + AHEAD))
        def _():
            wait_in((0, 15), s - AHEAD)
            start((2, 4, 17, 19, 8), s - AHEAD)

        @pl.when((s >= AHEAD + 1) & (s < PARTS + AHEAD + 1))
        def _():
            t = s - AHEAD - 1
            wait_in((1, 16), t)
            start((5, 20, 9), t)
            wait_in((4, 19), t)
            start((6, 21, 12), t)
            wait_in((2, 3), t)
            start((10, 11), t)

        @pl.when((s >= AHEAD + 2) & (s < PARTS + AHEAD + 2))
        def _():
            wait_in((5, 6), s - AHEAD - 2)
            start((13, 14), s - AHEAD - 2)

        @pl.when(s >= AHEAD + 3)
        def _():
            t = s - AHEAD - 3
            wait_in((17, 18, 20, 21, 7, 8, 9, 10, 11, 12, 13, 14), t)
            score_part(t)
            for flow, (ref, slot, device) in sends.items():
                copy(flow, ref, slot, t, device).wait_send()

        return 0

    lax.fori_loop(0, PARTS + AHEAD + 3, step, 0)

    scale_lead = jnp.sqrt(jnp.sum(e_lead[...], -1, keepdims=True) / (NX * NX * ENTRIES) + epsilon)
    ones = jnp.ones((8, 128), f32)
    across = lax.dot_general(ones, e_col[...], NT, precision=lax.Precision.HIGHEST, preferred_element_type=f32)
    scale_col = jnp.sqrt(across[:1] / (NX * NX * ENTRIES) + epsilon)
    e_lead[...] = jnp.broadcast_to(scale_lead, (96, 128))
    to_shift = shift[...]

    def some(b):
        found = []
        for u in range(0, 8, 2):
            values = []
            for a in (b * 8 + u, b * 8 + u + 1):
                values.append(gram_a[pl.ds(a, NX, stride=PITCH_A), :])
                values.append(gram_a[pl.ds(a + 96, NX, stride=PITCH_A), :])
                values.append(gram_b[pl.ds(a, NX, stride=PITCH_B), :])
            value = jnp.concatenate(values, 1)
            high = value.astype(bf16)
            low = (value - high.astype(f32)).astype(bf16)
            moved = jnp.dot(to_shift, jnp.concatenate([high, low], 0), preferred_element_type=f32)
            top = jnp.max(moved[:NX] + moved[NX:], axis=0, keepdims=True)
            found.extend([top[:, :384], top[:, 384:]])
        found = jnp.concatenate(found, 0)
        found = jnp.concatenate(
            [jnp.maximum(found[:, :128], found[:, 128:256]), jnp.maximum(found[:, 256:320], found[:, 320:])], 1
        )
        rows = pl.ds(pl.multiple_of(b * 8, 8), 8)
        scale = e_lead[rows, :]
        scale = jnp.concatenate([scale, scale[:, :64]], 1)
        out[rows, :] = found / (math.sqrt(NX * ENTRIES) * scale * scale_col)

    def best(b, _):
        for u in range(4):
            some(b * 4 + u)
        return 0

    lax.fori_loop(0, 96 // 32, best, 0)

    for e, device in enumerate(others):
        tell(e, my_row, device).wait_send()
        for group in range(GROUPS):
            hand(e, group, device[0], my_row, device).wait_send()


def scores_of(count, dest, crossings):
    vmem = pl.BlockSpec(memory_space=pltpu.VMEM)
    smem = pl.BlockSpec(memory_space=pltpu.SMEM)
    return pl.pallas_call(
        score_kernel,
        out_shape=jax.ShapeDtypeStruct((COLS * M, ROWS * M), f32),
        in_specs=[smem, smem, pl.BlockSpec(memory_space=pl.ANY)] + [vmem] * 4,
        out_specs=vmem,
        scratch_shapes=[
            pltpu.VMEM((BUCKETS * ROWS, ENTRIES, NX), bf16),
            pltpu.VMEM((BUCKETS * ROWS, PARTS, 16, ENTRIES), bf16),
            pltpu.VMEM((ROWS, GROUPS, BUCKETS, GROUP, 16, ENTRIES), bf16),
            *[pltpu.VMEM((ROWS, BUCKETS, GROUP, 16, ENTRIES), bf16)] * GROUPS,
            pltpu.SMEM((ROWS, 128), jnp.int32),
            pltpu.SMEM((BUCKETS * ROWS,), jnp.int32),
            pltpu.SMEM((M,), jnp.int32),
            pltpu.VMEM((ROWS, PARTS, M, 16, ENTRIES), bf16),
            pltpu.VMEM((COLS, PARTS, M, 16, ENTRIES), bf16),
            pltpu.VMEM((16, 192, ENTRIES), bf16),
            pltpu.VMEM((16, 192, ENTRIES), bf16),
            pltpu.VMEM((NX * PITCH_A, 128), f32),
            pltpu.VMEM((NX * PITCH_B, 128), f32),
            pltpu.VMEM((96, 128), f32),
            pltpu.VMEM((192, 128), f32),
            pltpu.SemaphoreType.DMA,
            pltpu.SemaphoreType.DMA((22, PARTS)),
            pltpu.SemaphoreType.DMA((22, PARTS)),
            pltpu.SemaphoreType.DMA((15, GROUPS)),
            pltpu.SemaphoreType.DMA((15, GROUPS)),
            pltpu.SemaphoreType.DMA((15,)),
            pltpu.SemaphoreType.DMA((15,)),
        ],
        compiler_params=pltpu.CompilerParams(
            collective_id=1, has_side_effects=True, vmem_limit_bytes=60 * 2**20
        ),
        name="scores",
    )(count, dest, crossings, *[jnp.asarray(table) for table in tables()])


def body(crossings, counts, dest):
    return scores_of(counts, dest, crossings.reshape(BUCKETS * ROWS, ENTRIES, NX))


def solution(mesh):
    return jax.shard_map(
        body,
        mesh=mesh,
        in_specs=(P(("row", "col"), None, None, None), P("col", "row"), P(("row", "col"), None)),
        out_specs=P("row", "col"),
        check_vma=False,
    )
```

```python
import math

import jax
import jax.numpy as jnp
import ml_dtypes
import numpy as np
from jax import lax
from jax.experimental import pallas as pl
from jax.experimental.pallas import tpu as pltpu
from jax.sharding import PartitionSpec as P

M = 12
NX = 128
ENTRIES = 256
ROWS = 16
COLS = 8
BUCKETS = 3
PARTS = 8
PITCH_A = 200
PITCH_B = 104
GROUP = 2
GROUPS = PARTS // GROUP
EARLY = 2
AHEAD = 3

epsilon = 1e-06

MESH = pl.DeviceIdType.MESH
NT = (((1,), (1,)), ((), ()))
f32 = jnp.float32
bf16 = jnp.bfloat16


def split3(table):
    high = table.astype(ml_dtypes.bfloat16)
    rest = table - high.astype(np.float64)
    mid = rest.astype(ml_dtypes.bfloat16)
    low = (rest - mid.astype(np.float64)).astype(ml_dtypes.bfloat16)
    return high, mid, low


def tables():
    rows = np.arange(NX)
    part, inner = rows // 16, rows % 16
    wave = part * 8 + inner % 8
    imaginary = (inner >= 8) & (wave > 0)
    wave = np.where((inner >= 8) & (wave == 0), NX // 2, wave)
    points = np.arange(NX)
    angles = 2.0 * math.pi * ((wave[:, None] * points[None, :]) % NX) / NX
    forward = np.where(imaginary[:, None], -np.sin(angles), np.cos(angles))
    weight = np.where((wave == 0) | (wave == NX // 2), 1.0, 2.0)[:, None]
    inverse = weight * np.where(imaginary[:, None], -np.sin(angles), np.cos(angles)) / NX
    inverse = inverse - inverse.mean(1, keepdims=True)
    f_high, f_mid, f_low = split3(forward)
    forward_stack = np.concatenate([f_high, f_mid, f_low], 0)
    i_high, i_mid, _ = split3(inverse.T)
    shift = np.block([[i_high, i_high], [i_mid, np.zeros_like(i_mid)]])
    swap = np.zeros((256, 256))
    for first in range(16):
        for second in range(16):
            swap[first * 16 + second, second * 16 + first] = 1.0
    mirror = np.zeros((ENTRIES, ENTRIES))
    for point in range(128):
        mirror[(-point) % 128, point] = 1.0
        mirror[128 + (-point) % 128, 128 + point] = -1.0
    return (
        forward_stack.astype(ml_dtypes.bfloat16),
        swap.astype(ml_dtypes.bfloat16),
        mirror.astype(ml_dtypes.bfloat16),
        shift.astype(ml_dtypes.bfloat16),
    )


def dot_nt(a, b):
    return lax.dot_general(a, b, NT, preferred_element_type=f32)


def place():
    r = lax.axis_index("row")
    c = lax.axis_index("col")
    return r // 8, (r // 2) % 4, r % 2, c // 2, c % 2


OTHERS = [
    (1, 2, 0), (1, 2, 1), (0, 2, 0), (0, 2, 1), (1, 1, 0), (1, 3, 0), (1, 1, 1), (1, 3, 1),
    (0, 1, 0), (0, 3, 0), (0, 1, 1), (0, 3, 1), (1, 0, 0), (1, 0, 1), (0, 0, 1),
]


def score_kernel(
    count, dest, crossings, forward, swap, mirror, shift, out,
    held, coeffs, staged, planes_0, planes_1, planes_2, planes_3, tally, slots, picks, cols, leads, y_lead, y_col, gram_a, gram_b, e_lead, e_col,
    load, send, recv, hand_out, hand_in, count_out, count_in,
):
    fetch = pltpu.make_async_copy(crossings, held, load)
    fetch.start()
    z, x, k, y, h = place()
    my_row = z * 8 + x * 2 + k
    my_col = y * 2 + h

    def row_at(dz, dx, dk=0):
        return ((z + dz) % 2) * 8 + ((x + dx) % 4) * 2 + (k + dk) % 2

    def col_at(dh, dy):
        return ((y + dy) % 4) * 2 + (h + dh) % 2

    sib, zl = (row_at(0, 0, 1), my_col), (row_at(1, 0), my_col)
    xp, xm = (row_at(0, 1), my_col), (row_at(0, 3), my_col)
    zh, yp, ym = (my_row, col_at(1, 0)), (my_row, col_at(0, 1)), (my_row, col_at(0, 3))

    barrier = pltpu.get_barrier_semaphore()
    others = [(row_at(*step), my_col) for step in OTHERS]
    for device in others + [zh, yp, ym]:
        pl.semaphore_signal(barrier, inc=1, device_id=device, device_id_type=MESH)
    tally[my_row, 0] = count[0, 0]
    pl.semaphore_wait(barrier, len(OTHERS) + 3)

    def tell(e, row, device):
        return pltpu.make_async_remote_copy(
            src_ref=tally.at[row],
            dst_ref=tally.at[row],
            send_sem=count_out.at[e],
            recv_sem=count_in.at[e],
            device_id=device,
            device_id_type=MESH,
        )

    planes = (planes_0, planes_1, planes_2, planes_3)

    def hand(e, group, row, source, device):
        return pltpu.make_async_remote_copy(
            src_ref=staged.at[row, group],
            dst_ref=planes[group].at[source],
            send_sem=hand_out.at[e, group],
            recv_sem=hand_in.at[e, group],
            device_id=device,
            device_id_type=MESH,
        )

    senders = [row_at(dz, -dx, dk) for dz, dx, dk in OTHERS]
    for e, device in enumerate(others):
        tell(e, my_row, device).start()
    fetch.wait()

    def prepare(b, _):
        for u in range(4):
            n = b * 4 + u
            slot = jnp.int32(0)
            for s in range(BUCKETS * ROWS):
                slot = jnp.where(dest[0, s] == n, s, slot)
            slots[n] = slot
            parts = dot_nt(forward[...], held[n])
            value = (parts[:NX] + (parts[NX : 2 * NX] + parts[2 * NX :])).astype(bf16)
            for t in range(PARTS):
                coeffs[n, t] = value[t * 16 : (t + 1) * 16]
        return 0

    lax.fori_loop(0, BUCKETS * ROWS // 4, prepare, 0)
    for e, device in enumerate(others):
        tell(e, senders[e], device).wait_recv()
    my_offset = jnp.int32(0)
    for r in range(ROWS):
        my_offset = my_offset + jnp.where(r < my_row, tally[r, 0], 0)

    def hand_over(group):
        for e, device in enumerate(others):
            target = device[0]
            for t in range(BUCKETS):
                slot = slots[t * ROWS + (target + 256 * ROWS - my_offset) % ROWS]
                for g in range(GROUP):
                    staged[target, group, t, g] = coeffs[slot, group * GROUP + g]
            hand(e, group, target, my_row, device).start()
        for t in range(BUCKETS):
            slot = slots[t * ROWS + (my_row + 256 * ROWS - my_offset) % ROWS]
            for g in range(GROUP):
                planes[group][my_row, t, g] = coeffs[slot, group * GROUP + g]

    def take(group):
        for e, device in enumerate(others):
            hand(e, group, device[0], senders[e], device).wait_recv()
        for p in range(M):
            source = picks[p]
            for g in range(GROUP):
                value = planes[group][source // BUCKETS, source % BUCKETS, g]
                cols[my_row, group * GROUP + g, p] = value
                leads[my_col, group * GROUP + g, p] = value

    for group in range(EARLY):
        hand_over(group)

    def pick(p, _):
        wanted = p * ROWS + my_row
        offset, found = jnp.int32(0), jnp.int32(0)
        for r in range(ROWS):
            within = wanted - offset
            hit = (within >= 0) & (within < tally[r, 0])
            found = jnp.where(hit, r * BUCKETS + within // ROWS, found)
            offset = offset + tally[r, 0]
        picks[p] = found
        return 0

    lax.fori_loop(0, M, pick, 0)

    def piece(ref, slot, t):
        return ref.at[slot, t]

    def copy(flow, ref, slot, t, device):
        block = piece(ref, slot, t)
        return pltpu.make_async_remote_copy(
            src_ref=block,
            dst_ref=block,
            send_sem=send.at[flow, t],
            recv_sem=recv.at[flow, t],
            device_id=device,
            device_id_type=MESH,
        )

    own_c, own_l = row_at(0, 0), col_at(0, 0)
    sends = {
        0: (cols, own_c, zl), 1: (cols, own_c, xp), 3: (cols, own_c, xm), 7: (cols, own_c, sib),
        2: (cols, row_at(1, 0), xp), 4: (cols, row_at(1, 0), xm), 8: (cols, row_at(1, 0), sib),
        5: (cols, row_at(0, 3), xp), 9: (cols, row_at(0, 3), sib), 10: (cols, row_at(1, 3), sib),
        11: (cols, row_at(0, 1), sib), 6: (cols, row_at(1, 1), xm), 12: (cols, row_at(1, 1), sib),
        13: (cols, row_at(0, 2), sib), 14: (cols, row_at(1, 2), sib),
        15: (leads, own_l, zh), 16: (leads, own_l, yp), 18: (leads, own_l, ym),
        17: (leads, col_at(1, 0), yp), 19: (leads, col_at(1, 0), ym),
        20: (leads, col_at(0, 3), yp), 21: (leads, col_at(1, 1), ym),
    }
    arrives = {
        0: row_at(1, 0), 1: row_at(0, 3), 2: row_at(1, 3), 3: row_at(0, 1), 4: row_at(1, 1),
        5: row_at(0, 2), 6: row_at(1, 2),
        7: row_at(0, 0, 1), 8: row_at(1, 0, 1), 9: row_at(0, 3, 1), 10: row_at(1, 3, 1),
        11: row_at(0, 1, 1), 12: row_at(1, 1, 1), 13: row_at(0, 2, 1), 14: row_at(1, 2, 1),
        15: col_at(1, 0), 16: col_at(0, 3), 17: col_at(1, 3), 18: col_at(0, 1), 19: col_at(1, 1),
        20: col_at(0, 2), 21: col_at(1, 2),
    }

    def start(flows, t):
        for flow in flows:
            ref, slot, device = sends[flow]
            copy(flow, ref, slot, t, device).start()

    def wait_in(flows, t):
        for flow in flows:
            ref, _, device = sends[flow]
            copy(flow, ref, arrives[flow], t, device).wait_recv()

    e_lead[...] = jnp.zeros_like(e_lead)
    e_col[...] = jnp.zeros_like(e_col)

    def score_part(t):
        order = swap[...]

        def relay(ref, groups, dst):
            for g in range(groups):
                block = jnp.concatenate([ref[b // M, t, b % M] for b in range(g * 16, (g + 1) * 16)], 0)
                turned = jnp.dot(order, block, preferred_element_type=f32).astype(bf16)
                dst[:, g * 16 : (g + 1) * 16, :] = turned.reshape(16, 16, ENTRIES)

        relay(leads, 6, y_lead)
        relay(cols, 12, y_col)
        first = jnp.where(t == 0, 1.0, 0.0).astype(f32)
        for dst, source, count in ((e_lead, y_lead, 96), (e_col, y_col, 192)):
            total = dst[...]
            for j in range(16):
                value = source[j, :count, :].astype(f32)
                square = value * value
                square = square[:, :128] + square[:, 128:]
                weight = (2.0 - first) if j % 8 == 0 else 2.0
                total = total + weight * square
            dst[...] = total
        turn = mirror[...]
        for j in range(16):
            y_lead[j, 96:, :] = jnp.dot(y_lead[j, :96, :], turn, preferred_element_type=f32).astype(bf16)
        for i in range(8):
            lr, li, tr, ti = y_lead[i], y_lead[8 + i], y_col[i], y_col[8 + i]
            both = jnp.concatenate([lr, li], 0)
            with_real, with_imag = dot_nt(both, tr), dot_nt(both, ti)
            rr, ir, ri, ii = with_real[:192], with_real[192:], with_imag[:192], with_imag[192:]
            if i == 0:
                real = rr + (1.0 - first) * ii
                imag = first * ii + (1.0 - first) * (ri - ir)
            else:
                real, imag = rr + ii, ri - ir
            for value, j in ((real, i), (imag, 8 + i)):
                gram_a[pl.ds(pl.multiple_of((t * 16 + j) * PITCH_A, 8), 192), :] = value[:, :128]
                pair = jnp.concatenate([value[:96, 128:], value[96:, 128:]], 1)
                gram_b[pl.ds(pl.multiple_of((t * 16 + j) * PITCH_B, 8), 96), :] = pair

    def step(s, _):
        for group in range(GROUPS):
            @pl.when(s == group * GROUP)
            def _():
                take(group)

        @pl.when(s < PARTS)
        def _():
            start((0, 1, 3, 15, 16, 18, 7), s)

        for group in range(EARLY, GROUPS):
            @pl.when(s == (group - EARLY) * GROUP + 1)
            def _():
                hand_over(group)

        @pl.when((s >= AHEAD) & (s < PARTS + AHEAD))
        def _():
            wait_in((0, 15), s - AHEAD)
            start((2, 4, 17, 19, 8), s - AHEAD)

        @pl.when((s >= AHEAD + 1) & (s < PARTS + AHEAD + 1))
        def _():
            t = s - AHEAD - 1
            wait_in((1, 16), t)
            start((5, 20, 9), t)
            wait_in((4, 19), t)
            start((6, 21, 12), t)
            wait_in((2, 3), t)
            start((10, 11), t)

        @pl.when((s >= AHEAD + 2) & (s < PARTS + AHEAD + 2))
        def _():
            wait_in((5, 6), s - AHEAD - 2)
            start((13, 14), s - AHEAD - 2)

        @pl.when(s >= AHEAD + 3)
        def _():
            t = s - AHEAD - 3
            wait_in((17, 18, 20, 21, 7, 8, 9, 10, 11, 12, 13, 14), t)
            score_part(t)
            for flow, (ref, slot, device) in sends.items():
                copy(flow, ref, slot, t, device).wait_send()

        return 0

    lax.fori_loop(0, PARTS + AHEAD + 3, step, 0)

    scale_lead = jnp.sqrt(jnp.sum(e_lead[...], -1, keepdims=True) / (NX * NX * ENTRIES) + epsilon)
    ones = jnp.ones((8, 128), f32)
    across = lax.dot_general(ones, e_col[...], NT, precision=lax.Precision.HIGHEST, preferred_element_type=f32)
    scale_col = jnp.sqrt(across[:1] / (NX * NX * ENTRIES) + epsilon)
    e_lead[...] = jnp.broadcast_to(scale_lead, (96, 128))
    to_shift = shift[...]

    def some(b):
        found = []
        for u in range(0, 8, 2):
            values = []
            for a in (b * 8 + u, b * 8 + u + 1):
                values.append(gram_a[pl.ds(a, NX, stride=PITCH_A), :])
                values.append(gram_a[pl.ds(a + 96, NX, stride=PITCH_A), :])
                values.append(gram_b[pl.ds(a, NX, stride=PITCH_B), :])
            value = jnp.concatenate(values, 1)
            high = value.astype(bf16)
            low = (value - high.astype(f32)).astype(bf16)
            moved = jnp.dot(to_shift, jnp.concatenate([high, low], 0), preferred_element_type=f32)
            top = jnp.max(moved[:NX] + moved[NX:], axis=0, keepdims=True)
            found.extend([top[:, :384], top[:, 384:]])
        found = jnp.concatenate(found, 0)
        found = jnp.concatenate(
            [jnp.maximum(found[:, :128], found[:, 128:256]), jnp.maximum(found[:, 256:320], found[:, 320:])], 1
        )
        rows = pl.ds(pl.multiple_of(b * 8, 8), 8)
        scale = e_lead[rows, :]
        scale = jnp.concatenate([scale, scale[:, :64]], 1)
        out[rows, :] = found / (math.sqrt(NX * ENTRIES) * scale * scale_col)

    def best(b, _):
        for u in range(6):
            some(b * 6 + u)
        return 0

    lax.fori_loop(0, 96 // 48, best, 0)

    for e, device in enumerate(others):
        tell(e, my_row, device).wait_send()
        for group in range(GROUPS):
            hand(e, group, device[0], my_row, device).wait_send()


def scores_of(count, dest, crossings):
    vmem = pl.BlockSpec(memory_space=pltpu.VMEM)
    smem = pl.BlockSpec(memory_space=pltpu.SMEM)
    return pl.pallas_call(
        score_kernel,
        out_shape=jax.ShapeDtypeStruct((COLS * M, ROWS * M), f32),
        in_specs=[smem, smem, pl.BlockSpec(memory_space=pl.ANY)] + [vmem] * 4,
        out_specs=vmem,
        scratch_shapes=[
            pltpu.VMEM((BUCKETS * ROWS, ENTRIES, NX), bf16),
            pltpu.VMEM((BUCKETS * ROWS, PARTS, 16, ENTRIES), bf16),
            pltpu.VMEM((ROWS, GROUPS, BUCKETS, GROUP, 16, ENTRIES), bf16),
            *[pltpu.VMEM((ROWS, BUCKETS, GROUP, 16, ENTRIES), bf16)] * GROUPS,
            pltpu.SMEM((ROWS, 128), jnp.int32),
            pltpu.SMEM((BUCKETS * ROWS,), jnp.int32),
            pltpu.SMEM((M,), jnp.int32),
            pltpu.VMEM((ROWS, PARTS, M, 16, ENTRIES), bf16),
            pltpu.VMEM((COLS, PARTS, M, 16, ENTRIES), bf16),
            pltpu.VMEM((16, 192, ENTRIES), bf16),
            pltpu.VMEM((16, 192, ENTRIES), bf16),
            pltpu.VMEM((NX * PITCH_A, 128), f32),
            pltpu.VMEM((NX * PITCH_B, 128), f32),
            pltpu.VMEM((96, 128), f32),
            pltpu.VMEM((192, 128), f32),
            pltpu.SemaphoreType.DMA,
            pltpu.SemaphoreType.DMA((22, PARTS)),
            pltpu.SemaphoreType.DMA((22, PARTS)),
            pltpu.SemaphoreType.DMA((15, GROUPS)),
            pltpu.SemaphoreType.DMA((15, GROUPS)),
            pltpu.SemaphoreType.DMA((15,)),
            pltpu.SemaphoreType.DMA((15,)),
        ],
        compiler_params=pltpu.CompilerParams(
            collective_id=1, has_side_effects=True, vmem_limit_bytes=60 * 2**20
        ),
        name="scores",
    )(count, dest, crossings, *[jnp.asarray(table) for table in tables()])


def body(crossings, counts, dest):
    return scores_of(counts, dest, crossings.reshape(BUCKETS * ROWS, ENTRIES, NX))


def solution(mesh):
    return jax.shard_map(
        body,
        mesh=mesh,
        in_specs=(P(("row", "col"), None, None, None), P("col", "row"), P(("row", "col"), None)),
        out_specs=P("row", "col"),
        check_vma=False,
    )
```
